512 devices in a mesh: section: 16 (over z_hi, y, core), tensor: 32 (over z_lo, x).
Axes of the slice: x: 4, y: 4, z: 16 (z_hi: 2, z_lo: 8; z = z_hi * 8 + z_lo), core: 2. Of those that a mesh axis runs over, the one named last changes fastest.
Arguments:
- encoded: bfloat16 [16, 256, 8192], P(None, 'section', 'tensor'), may hold values from -6 to 6
- w_key: bfloat16 [16, 8192, 4096], P('section', None, 'tensor'), may hold values from -0.125 to 0.125
- w_value: bfloat16 [16, 8192, 4096], P('section', None, 'tensor'), may hold values from -0.0625 to 0.0625
- queries: bfloat16 [16, 64, 4096], P('section', None, 'tensor'), may hold values from -6 to 6
- cotangent: bfloat16 [16, 64, 4096], P('section', None, 'tensor'), may hold values from -96 to 96
- counts: int32 [16, 1], P('section'), may hold values from 0 to 2
Outputs:
- grad_query: bfloat16 [16, 64, 4096], P('section', None, 'tensor')
- grad_encoded: float32 [16, 256, 8192], P(None, 'section', 'tensor')
The draws below stay inside these ranges and needn't reach their ends.
All inputs are finite; a program needn't handle non-finite values.
Results may differ from the reference program's by a relative error of at most 0.03.
Values may be sent and summed in bfloat16 or wider, within the bound.
No kernel may reach another device: no remote copies, remote signals or barrier semaphores. Data moves between devices by JAX's collectives and lax.ppermute only.
A program may use at most 64 MiB of HBM per device.

```python
import math
import jax
import jax.numpy as jnp
from jax import lax

D = 8192
HD = 128
GROUP = 64
NBR_LEN = 128
NBRS = 2
GROUPS = 1
HEADS = 32
MB = 16
TOKS = 64
NROWS = 256


def place_ends(entries, stream_key, smallest, largest):
    dims = entries.shape
    spot = [jax.random.randint(jax.random.fold_in(stream_key, axis), (), 0, dims[axis]) for axis in range(len(dims))]
    entries = entries.at[tuple(spot)].set(smallest)
    longest = dims.index(max(dims))
    spot[longest] = (spot[longest] + 1) % dims[longest]
    return entries.at[tuple(spot)].set(largest)


def raised(values, key, source, target, parts, factor):
    def block_of(axis_at):
        return (jnp.arange(values.shape[axis_at]) // (values.shape[axis_at] // parts)).reshape((-1,) + (1,) * (values.ndim - 1 - axis_at))

    near = jax.random.permutation(key, parts)[block_of(target)]
    far = (block_of(target) + parts // 2) % parts
    return jnp.where((block_of(source) == near) | (block_of(source) == far), factor * values, values)


def levels(own_key, extent, pieces, least, largest):
    def one(position, blocks):
        heights = jax.random.uniform(jax.random.fold_in(jax.random.fold_in(own_key, 6), position), (blocks,), jnp.float32, least / len(pieces), largest / len(pieces))
        return jnp.repeat(jnp.exp(heights), extent[position] // blocks).reshape((-1,) + (1,) * (len(extent) - position - 1))

    gain = one(*pieces[0])
    for cut in pieces[1:]:
        gain = gain * one(*cut)
    return gain


def bell_draw(stream_key, dims, deviation, most, split=(), kind=jnp.bfloat16):
    drawn = jax.random.normal(stream_key, dims, jnp.float32) * deviation
    if len(split) > 0:
        drawn = levels(stream_key, dims, split, -0.22, 0.18) * drawn
    return jnp.clip(drawn, min=-most, max=most).astype(kind)


def noise_with(own_key, shape, spread, most, pieces, heavy, kind=jnp.bfloat16):
    array = spread * jax.random.normal(own_key, shape, jnp.float32)
    if pieces:
        array = array * levels(own_key, shape, pieces, -0.22, 0.18)
    return jnp.clip(raised(array, jax.random.fold_in(own_key, 3), *heavy), -most, most).astype(kind)


def setup_inputs(seed: int = 0) -> dict:
    keys = jax.random.split(jax.random.key(seed), 7)
    return {
        "encoded": bell_draw(keys[0], (MB, NROWS, D), 1.0, 6.0, ((1, 16), (2, 32))),
        "w_key": noise_with(keys[1], (MB, D, HEADS * HD), D ** -0.5, 0.125, ((0, 16), (2, 32)), (2, 1, 32, 2.75)),
        "w_value": bell_draw(keys[2], (MB, D, HEADS * HD), D ** -0.5, 0.0625, ((0, 16), (2, 32))),
        "queries": bell_draw(keys[3], (MB, TOKS, HEADS * HD), 1.0, 6.0, ((0, 16), (2, 32))),
        "cotangent": bell_draw(keys[4], (MB, TOKS, HEADS * HD), 16.0, 96.0, ((0, 16), (2, 32))),
        "counts": place_ends(jax.random.randint(keys[5], (MB, GROUPS), 0, NBRS + 1), jax.random.fold_in(keys[5], 1), 0, NBRS).astype(jnp.int32),
    }


def head_backward(encoder_rows, key_weight, value_weight, query_block, grad_block, live_mask, no_neighbours):
    width_head = key_weight.shape[1]
    inverse_root = 1.0 / math.sqrt(width_head)
    group_count = query_block.shape[0]
    key_rows = jnp.dot(encoder_rows, key_weight, preferred_element_type=jnp.float32).astype(jnp.bfloat16)
    value_rows = jnp.dot(encoder_rows, value_weight, preferred_element_type=jnp.float32).astype(jnp.bfloat16)
    key_blocks = key_rows.reshape(group_count, -1, width_head).astype(jnp.float32)
    value_blocks = value_rows.reshape(group_count, -1, width_head).astype(jnp.float32)
    query_wide = query_block.astype(jnp.float32)
    grad_wide = grad_block.astype(jnp.float32)
    scores = jnp.einsum('cqd,ckd->cqk', query_wide, key_blocks) * inverse_root
    weighted = jnp.where(live_mask[:, None, :] > 0.5, jnp.exp(scores), 0.0)
    totals = lax.optimization_barrier(jnp.sum(weighted, axis=2, keepdims=True)) + no_neighbours[:, None, None]
    probs = weighted / totals
    probs_low = probs.astype(jnp.bfloat16).astype(jnp.float32)
    grad_values = jnp.einsum('cqk,cqd->ckd', probs_low, grad_wide).astype(jnp.bfloat16)
    grad_probs = jnp.einsum('cqd,ckd->cqk', grad_wide, value_blocks)
    centre = lax.optimization_barrier(jnp.sum(probs * grad_probs, axis=2, keepdims=True))
    grad_scores = (probs * (grad_probs - centre)).astype(jnp.bfloat16).astype(jnp.float32)
    grad_queries = (jnp.einsum('cqk,ckd->cqd', grad_scores, key_blocks) * inverse_root).astype(jnp.bfloat16)
    grad_keys = (jnp.einsum('cqk,cqd->ckd', grad_scores, query_wide) * inverse_root).astype(jnp.bfloat16)
    head_term = jnp.dot(grad_keys.reshape(-1, width_head), key_weight.T, preferred_element_type=jnp.float32)
    head_term = head_term + jnp.dot(grad_values.reshape(-1, width_head), value_weight.T, preferred_element_type=jnp.float32)
    return (grad_queries.reshape(-1, width_head), head_term.astype(jnp.bfloat16))

def reference(encoded, w_key, w_value, queries, cotangent, counts):
    slot_index = jnp.arange(NBRS * NBR_LEN, dtype=jnp.int32) // NBR_LEN
    query_grads = []
    encoder_grads = []
    for layer_index in range(MB):
        own_counts = counts[layer_index]
        live_mask = (slot_index[None, :] < own_counts[:, None]).astype(jnp.float32)
        no_neighbours = (own_counts == 0).astype(jnp.float32)
        key_heads = jnp.moveaxis(w_key[layer_index].reshape(D, HEADS, HD), 1, 0)
        value_heads = jnp.moveaxis(w_value[layer_index].reshape(D, HEADS, HD), 1, 0)
        query_heads = jnp.moveaxis(queries[layer_index].reshape(GROUPS, GROUP, HEADS, HD), 2, 0)
        grad_heads = jnp.moveaxis(cotangent[layer_index].reshape(GROUPS, GROUP, HEADS, HD), 2, 0)
        encoder_rows = encoded[layer_index]

        def per_head(running, inputs_tuple):
            key_weight, value_weight, query_block, grad_block = inputs_tuple
            grad_queries, head_term = head_backward(encoder_rows, key_weight, value_weight, query_block, grad_block, live_mask, no_neighbours)
            return (running + head_term.astype(jnp.float32), grad_queries)
        running, head_queries = lax.scan(per_head, jnp.zeros((NROWS, D), jnp.float32), (key_heads, value_heads, query_heads, grad_heads))
        encoder_grads.append(running)
        query_grads.append(jnp.moveaxis(head_queries, 0, 1).reshape(TOKS, HEADS * HD))
    return (jnp.stack(query_grads), jnp.stack(encoder_grads))
```

```python
import math

import jax
import jax.numpy as jnp
from jax import lax
from jax.experimental import pallas as pl
from jax.experimental.pallas import tpu as pltpu
from jax.sharding import Mesh, PartitionSpec as P

NBR_LEN = 128
HEAD = 128
GROUP = 64
BLOCK = 256
INV = 1.0 / math.sqrt(HEAD)
F32 = jnp.float32
BF16 = jnp.bfloat16

SECTION = ("zh", "y", "c")
TENSOR = ("z4", "z2", "x")
TEAM = ("z2", "x")
SPREAD = ("zh", "y", "c", "z4")


def nt(a, b):
    return lax.dot_general(a, b, (((1,), (1,)), ((), ())), preferred_element_type=F32)


def project_kernel(q_ref, ct_ref, wk_ref, wv_ref, out_ref):
    for d in range(out_ref.shape[0]):
        for a in range(wk_ref.shape[0]):
            cols = pl.ds(a * BLOCK, BLOCK)
            out_ref[d, 0:GROUP, cols] = nt(q_ref[...], wk_ref[a, d]).astype(BF16)
            out_ref[d, GROUP : 2 * GROUP, cols] = nt(ct_ref[...], wv_ref[a, d]).astype(BF16)


def project(q, ct, wk, wv):
    per = 2
    w_spec = pl.BlockSpec((4, per, BLOCK, HEAD), lambda i: (0, i, 0, 0))
    small = pl.BlockSpec((GROUP, HEAD), lambda i: (0, 0))
    return pl.pallas_call(
        project_kernel,
        grid=(8 // per,),
        in_specs=[small, small, w_spec, w_spec],
        out_specs=pl.BlockSpec((per, 2 * GROUP, 4 * BLOCK), lambda i: (i, 0, 0)),
        out_shape=jax.ShapeDtypeStruct((8, 2 * GROUP, 4 * BLOCK), BF16),
        cost_estimate=pl.CostEstimate(
            flops=2 * 128 * 8192 * 128, bytes_accessed=6 << 20, transcendentals=0
        ),
    )(q, ct, wk.reshape(4, 8, BLOCK, HEAD), wv.reshape(4, 8, BLOCK, HEAD))


def score_kernel(a_ref, e_ref, out_ref):
    total = None
    rows = a_ref.shape[0] * a_ref.shape[1]
    for b in range(4):
        part = nt(
            a_ref[:, :, b * BLOCK : (b + 1) * BLOCK].reshape(rows, BLOCK),
            e_ref[:, b].reshape(256, BLOCK),
        )
        total = part if total is None else total + part
    out_ref[...] = total.astype(BF16).reshape(out_ref.shape)


def score(a, e):
    per = 2
    return pl.pallas_call(
        score_kernel,
        grid=(8 // per,),
        in_specs=[
            pl.BlockSpec((per, 2 * GROUP, 4 * BLOCK), lambda i: (i, 0, 0)),
            pl.BlockSpec((16, 4, 16, BLOCK), lambda i: (0, 0, 0, 0)),
        ],
        out_specs=pl.BlockSpec((per, 2 * GROUP, 256), lambda i: (i, 0, 0)),
        out_shape=jax.ShapeDtypeStruct((8, 2 * GROUP, 256), BF16),
        cost_estimate=pl.CostEstimate(
            flops=2 * 1024 * 1024 * 256, bytes_accessed=3 << 20, transcendentals=0
        ),
    )(a, e)


def attend_kernel(count_ref, s_ref, out_ref):
    total = s_ref[0].astype(F32)
    for k in range(1, 8):
        total = total + s_ref[k].astype(F32)
    scores = total[0:GROUP] * INV
    grad_probs = total[GROUP : 2 * GROUP]
    count = count_ref[0]
    row = lax.broadcasted_iota(jnp.int32, scores.shape, 1)
    weighted = jnp.where(row < count * NBR_LEN, jnp.exp(scores), 0.0)
    empty = jnp.where(count == 0, 1.0, 0.0)
    probs = weighted / (jnp.sum(weighted, axis=1, keepdims=True) + empty)
    centre = jnp.sum(probs * grad_probs, axis=1, keepdims=True)
    grad_scores = (probs * (grad_probs - centre) * INV).astype(BF16)
    probs_low = probs.astype(BF16)
    for k in range(8):
        out_ref[k, 0:GROUP] = grad_scores
        out_ref[k, GROUP : 2 * GROUP] = probs_low


def attend(counts, s):
    return pl.pallas_call(
        attend_kernel,
        in_specs=[
            pl.BlockSpec(memory_space=pltpu.SMEM),
            pl.BlockSpec(memory_space=pltpu.VMEM),
        ],
        out_specs=pl.BlockSpec(memory_space=pltpu.VMEM),
        out_shape=jax.ShapeDtypeStruct((8, 2 * GROUP, 256), BF16),
    )(counts, s)


def term_kernel(g_ref, a_ref, out_ref, gt_ref):
    @pl.when(pl.program_id(0) == 0)
    def _():
        for h in range(8):
            gt_ref[:, h * 128 : (h + 1) * 128] = g_ref[h].astype(F32).T.astype(BF16)

    part = jnp.dot(
        gt_ref[...], a_ref[...].reshape(1024, BLOCK), preferred_element_type=F32
    )
    out_ref[:, 0] = part.astype(BF16).reshape(16, 16, BLOCK)


def term(g, a):
    return pl.pallas_call(
        term_kernel,
        grid=(4,),
        in_specs=[
            pl.BlockSpec((8, 2 * GROUP, 256), lambda i: (0, 0, 0)),
            pl.BlockSpec((8, 2 * GROUP, BLOCK), lambda i: (0, 0, i)),
        ],
        out_specs=pl.BlockSpec((16, 1, 16, BLOCK), lambda i: (0, i, 0, 0)),
        out_shape=jax.ShapeDtypeStruct((16, 4, 16, BLOCK), BF16),
        scratch_shapes=[pltpu.VMEM((256, 1024), BF16)],
        cost_estimate=pl.CostEstimate(
            flops=2 * 1024 * 1024 * 256, bytes_accessed=3 << 20, transcendentals=0
        ),
    )(g, a)


def mix_kernel(g_ref, e_ref, out_ref):
    gs = g_ref[:, 0:GROUP].reshape(8 * GROUP, 256)
    for b in range(4):
        part = jnp.dot(gs, e_ref[:, b].reshape(256, BLOCK), preferred_element_type=F32)
        out_ref[:, :, b * BLOCK : (b + 1) * BLOCK] = part.astype(BF16).reshape(8, GROUP, BLOCK)


def mix(g, e):
    vmem = pl.BlockSpec(memory_space=pltpu.VMEM)
    return pl.pallas_call(
        mix_kernel,
        in_specs=[vmem, vmem],
        out_specs=vmem,
        out_shape=jax.ShapeDtypeStruct((8, GROUP, 4 * BLOCK), BF16),
        cost_estimate=pl.CostEstimate(
            flops=2 * 512 * 256 * 1024, bytes_accessed=2 << 20, transcendentals=0
        ),
    )(g, e)


def query_kernel(x_ref, w_ref, out_ref, acc_ref):
    @pl.when(pl.program_id(0) == 0)
    def _():
        acc_ref[...] = jnp.zeros_like(acc_ref)

    total = acc_ref[...]
    for d in range(x_ref.shape[0]):
        for b in range(4):
            total = total + jnp.dot(
                x_ref[d, :, b * BLOCK : (b + 1) * BLOCK], w_ref[b, d], preferred_element_type=F32
            )
    acc_ref[...] = total
    out_ref[...] = total.astype(BF16)


def query(x, wk):
    per = 4
    return pl.pallas_call(
        query_kernel,
        grid=(8 // per,),
        in_specs=[
            pl.BlockSpec((per, GROUP, 4 * BLOCK), lambda i: (i, 0, 0)),
            pl.BlockSpec((4, per, BLOCK, HEAD), lambda i: (0, i, 0, 0)),
        ],
        out_specs=pl.BlockSpec((GROUP, HEAD), lambda i: (0, 0)),
        out_shape=jax.ShapeDtypeStruct((GROUP, HEAD), BF16),
        scratch_shapes=[pltpu.VMEM((GROUP, HEAD), F32)],
        cost_estimate=pl.CostEstimate(
            flops=2 * 64 * 8192 * 128, bytes_accessed=3 << 20, transcendentals=0
        ),
    )(x, wk.reshape(4, 8, BLOCK, HEAD))


def local(encoded, w_key, w_value, queries, cotangent, counts):
    key_weight, value_weight = w_key[0], w_value[0]
    out_rows = jnp.broadcast_to(encoded[:, None], (16, 4, 16, BLOCK)).reshape(64, 16, BLOCK)
    rows = lax.all_to_all(out_rows, SPREAD, 0, 0, tiled=True).reshape(16, 4, 16, BLOCK)
    projected = project(queries[0], cotangent[0], key_weight, value_weight)
    shared = lax.all_to_all(projected, TEAM, 0, 0, tiled=True)
    parts = lax.all_to_all(score(shared, rows), TEAM, 0, 0, tiled=True)
    grads = lax.all_to_all(attend(counts.reshape(1), parts), TEAM, 0, 0, tiled=True)
    sent = term(grads, shared).reshape(64, 16, BLOCK)
    terms = lax.all_to_all(sent, SPREAD, 0, 0, tiled=True).reshape(16, 4, 16, BLOCK)
    mixed = lax.all_to_all(mix(grads, rows), TEAM, 0, 0, tiled=True)
    grad_queries = query(mixed, key_weight)
    grad_encoded = jnp.sum(terms.astype(F32), axis=1)
    return grad_queries[None], grad_encoded


def solution(mesh):
    fine = Mesh(mesh.devices.reshape(2, 4, 2, 4, 2, 4), ("zh", "y", "c", "z4", "z2", "x"))
    by_head = P(SECTION, None, TENSOR)
    return jax.shard_map(
        local,
        mesh=fine,
        in_specs=(P(None, SECTION, TENSOR), by_head, by_head, by_head, by_head, P(SECTION, None)),
        out_specs=(by_head, P(None, SECTION, TENSOR)),
        check_vma=False,
    )
```

```python
import math

import jax
import jax.numpy as jnp
from jax import lax
from jax.experimental import pallas as pl
from jax.experimental.pallas import tpu as pltpu
from jax.sharding import Mesh, PartitionSpec as P

NBR_LEN = 128
HEAD = 128
GROUP = 64
PAIR = 2 * GROUP
ROWS = 256
BLOCK = 256
HALF = 4 * BLOCK
INV = 1.0 / math.sqrt(HEAD)
F32 = jnp.float32
BF16 = jnp.bfloat16

SECTION = ("zh", "y", "c")
TENSOR = ("z4", "z2", "x")
SPREAD = ("zh", "y", "c", "z4")
FLIP = [(0, 1), (1, 0)]


def across(k):
    return [(i, i ^ k) for i in range(4)]


def nt(a, b):
    return lax.dot_general(a, b, (((1,), (1,)), ((), ())), preferred_element_type=F32)


def nn(a, b):
    return jnp.dot(a, b, preferred_element_type=F32)


def cost(flops, nbytes):
    return pl.CostEstimate(flops=flops, bytes_accessed=nbytes, transcendentals=0)


def full(shape):
    return pl.BlockSpec(shape, lambda i, s: (0,) * len(shape))


def call(kernel, scalars, grid, in_specs, out_specs, out_shape, args, estimate, scratch=()):
    return pl.pallas_call(
        kernel,
        grid_spec=pltpu.PrefetchScalarGridSpec(
            num_scalar_prefetch=1,
            grid=(grid,),
            in_specs=in_specs,
            out_specs=out_specs,
            scratch_shapes=scratch,
        ),
        out_shape=out_shape,
        cost_estimate=estimate,
    )(scalars, *args)


def project_kernel(s_ref, q_ref, ct_ref, wk_ref, wv_ref, out_ref):
    for b in range(4):
        cols = pl.ds(b * BLOCK, BLOCK)
        out_ref[0:GROUP, cols] = nt(q_ref[...], wk_ref[b, 0, 0]).astype(BF16)
        out_ref[GROUP:PAIR, cols] = nt(ct_ref[...], wv_ref[b, 0, 0]).astype(BF16)


def project(scalars, q, ct, wk, wv, k):
    w_spec = pl.BlockSpec((4, 1, 1, BLOCK, HEAD), lambda i, s: (0, i, s[1] ^ k, 0, 0))
    small = full((GROUP, HEAD))
    return call(
        project_kernel,
        scalars,
        2,
        [small, small, w_spec, w_spec],
        pl.BlockSpec((PAIR, HALF), lambda i, s: (0, i)),
        jax.ShapeDtypeStruct((PAIR, 2 * HALF), BF16),
        (q, ct, wk, wv),
        cost(2 * 128 * 2048 * 128, 3 << 19),
    )


def partial_scores(a_refs, e_ref):
    total = None
    for b in range(4):
        a = jnp.concatenate([r[:, b * BLOCK : (b + 1) * BLOCK] for r in a_refs], axis=0)
        part = nt(a, e_ref[:, b].reshape(ROWS, BLOCK))
        total = part if total is None else total + part
    return total


def first_scores_kernel(s_ref, a0, a1, a2, a3, e_ref, out_ref):
    out_ref[...] = partial_scores((a0, a1, a2, a3), e_ref)


def last_scores_kernel(s_ref, a0, a1, a2, a3, e_ref, first_ref, out_ref):
    total = first_ref[...] + partial_scores((a0, a1, a2, a3), e_ref)
    for k in range(4):
        out_ref[s_ref[1] ^ k] = total[k * PAIR : (k + 1) * PAIR].astype(BF16)


A_OWN = pl.BlockSpec((PAIR, HALF), lambda i, s: (0, s[0]))
A_OTHER = pl.BlockSpec((PAIR, HALF), lambda i, s: (0, 1 - s[0]))
E_SPEC = full((16, 4, 16, BLOCK))
SCORE_COST = cost(2 * 512 * 1024 * 256, 2 << 20)


def first_scores(scalars, a, e):
    return call(
        first_scores_kernel,
        scalars,
        1,
        [A_OWN] * 4 + [E_SPEC],
        full((4 * PAIR, ROWS)),
        jax.ShapeDtypeStruct((4 * PAIR, ROWS), F32),
        (*a, e),
        SCORE_COST,
    )


def last_scores(scalars, a, e, first):
    return call(
        last_scores_kernel,
        scalars,
        1,
        [A_OTHER] * 4 + [E_SPEC, full((4 * PAIR, ROWS))],
        full((4, PAIR, ROWS)),
        jax.ShapeDtypeStruct((4, PAIR, ROWS), BF16),
        (*a, e, first),
        SCORE_COST,
    )


def attend_kernel(count_ref, s_ref, out_ref):
    total = s_ref[0].astype(F32)
    for k in range(1, 4):
        total = total + s_ref[k].astype(F32)
    scores = total[0:GROUP] * INV
    grad_probs = total[GROUP:PAIR]
    count = count_ref[0]
    row = lax.broadcasted_iota(jnp.int32, scores.shape, 1)
    weighted = jnp.where(row < count * NBR_LEN, jnp.exp(scores), 0.0)
    empty = jnp.where(count == 0, 1.0, 0.0)
    probs = weighted / (jnp.sum(weighted, axis=1, keepdims=True) + empty)
    centre = jnp.sum(probs * grad_probs, axis=1, keepdims=True)
    grad_scores = probs * (grad_probs - centre) * INV
    both = jnp.concatenate([grad_scores, probs], axis=0).T.astype(BF16)
    for k in range(4):
        out_ref[k] = both


def attend(counts, s):
    return pl.pallas_call(
        attend_kernel,
        in_specs=[
            pl.BlockSpec(memory_space=pltpu.SMEM),
            pl.BlockSpec(memory_space=pltpu.VMEM),
        ],
        out_specs=pl.BlockSpec(memory_space=pltpu.VMEM),
        out_shape=jax.ShapeDtypeStruct((4, ROWS, PAIR), BF16),
    )(counts, s)


def term_kernel(s_ref, g_ref, a0, a1, a2, a3, out_ref):
    g = jnp.concatenate([g_ref[s_ref[1] ^ k] for k in range(4)], axis=1)
    for b in range(4):
        a = jnp.concatenate([r[:, b * BLOCK : (b + 1) * BLOCK] for r in (a0, a1, a2, a3)], axis=0)
        out_ref[:, b] = nn(g, a).astype(out_ref.dtype).reshape(16, 16, BLOCK)


def term(scalars, g, a, a_spec, kind):
    return call(
        term_kernel,
        scalars,
        1,
        [full((4, ROWS, PAIR))] + [a_spec] * 4,
        E_SPEC,
        jax.ShapeDtypeStruct((16, 4, 16, BLOCK), kind),
        (g, *a),
        cost(2 * 512 * 1024 * 256, 2 << 20),
    )


def mix_kernel(s_ref, g_ref, own_ref, other_ref, *out_refs):
    gs = jnp.concatenate([g_ref[s_ref[1] ^ k, :, 0:GROUP] for k in range(4)], axis=1)
    gs = gs.astype(F32).T.astype(BF16)
    for p, e_ref in enumerate((own_ref, other_ref)):
        for b in range(4):
            part = nn(gs, e_ref[:, b].reshape(ROWS, BLOCK)).astype(BF16)
            for k in range(4):
                at = p * HALF + b * BLOCK
                out_refs[k][:, at : at + BLOCK] = part[k * GROUP : (k + 1) * GROUP]


def mix(scalars, g, own, other):
    return call(
        mix_kernel,
        scalars,
        1,
        [full((4, ROWS, PAIR)), E_SPEC, E_SPEC],
        [full((GROUP, 2 * HALF))] * 4,
        [jax.ShapeDtypeStruct((GROUP, 2 * HALF), BF16)] * 4,
        (g, own, other),
        cost(2 * 256 * 256 * 2048, 2 << 20),
    )


def query_kernel(s_ref, x0, x1, x2, x3, w_ref, out_ref, acc_ref):
    total = None
    for k, x_ref in enumerate((x0, x1, x2, x3)):
        for b in range(4):
            part = nn(x_ref[:, b * BLOCK : (b + 1) * BLOCK], w_ref[b, 0, s_ref[1] ^ k])
            total = part if total is None else total + part

    @pl.when(pl.program_id(0) == 0)
    def _():
        acc_ref[...] = total

    @pl.when(pl.program_id(0) == 1)
    def _():
        out_ref[...] = (acc_ref[...] + total).astype(BF16)


def query(scalars, x, wk):
    return call(
        query_kernel,
        scalars,
        2,
        [pl.BlockSpec((GROUP, HALF), lambda i, s: (0, i))] * 4
        + [pl.BlockSpec((4, 1, 4, BLOCK, HEAD), lambda i, s: (0, s[0] ^ i, 0, 0, 0))],
        full((GROUP, HEAD)),
        jax.ShapeDtypeStruct((GROUP, HEAD), BF16),
        (*x, wk),
        cost(2 * 64 * 8192 * 128, 3 << 20),
        [pltpu.VMEM((GROUP, HEAD), F32)],
    )


def to_members(parts):
    return [parts[0]] + [lax.ppermute(parts[k], "x", across(k)) for k in range(1, 4)]


def local(encoded, w_key, w_value, queries, cotangent, counts):
    scalars = jnp.stack([lax.axis_index("z2"), lax.axis_index("x")]).astype(jnp.int32)
    wk = w_key.reshape(4, 2, 4, BLOCK, HEAD)
    wv = w_value.reshape(4, 2, 4, BLOCK, HEAD)
    out_rows = jnp.broadcast_to(encoded[:, None], (16, 4, 16, BLOCK)).reshape(64, 16, BLOCK)
    own = lax.all_to_all(out_rows, SPREAD, 0, 0, tiled=True).reshape(16, 4, 16, BLOCK)
    shared = to_members(
        [project(scalars, queries[0], cotangent[0], wk, wv, k) for k in range(4)]
    )
    other = lax.ppermute(own, "z2", FLIP)
    first = first_scores(scalars, shared, own)
    sums = last_scores(scalars, shared, other, first)
    parts = lax.all_to_all(sums, "x", 0, 0, tiled=True)
    grads = lax.all_to_all(attend(counts.reshape(1), parts), "x", 0, 0, tiled=True)
    passed = lax.ppermute(term(scalars, grads, shared, A_OTHER, BF16), "z2", FLIP)
    kept = term(scalars, grads, shared, A_OWN, F32)
    sent = (kept + passed.astype(F32)).astype(BF16).reshape(64, 16, BLOCK)
    terms = lax.all_to_all(sent, SPREAD, 0, 0, tiled=True).reshape(16, 4, 16, BLOCK)
    mixed = to_members(mix(scalars, grads, own, other))
    grad_queries = query(scalars, mixed, wk)
    grad_encoded = jnp.sum(terms.astype(F32), axis=1)
    return grad_queries[None], grad_encoded


def solution(mesh):
    fine = Mesh(mesh.devices.reshape(2, 4, 2, 4, 2, 4), ("zh", "y", "c", "z4", "z2", "x"))
    by_head = P(SECTION, None, TENSOR)
    return jax.shard_map(
        local,
        mesh=fine,
        in_specs=(P(None, SECTION, TENSOR), by_head, by_head, by_head, by_head, P(SECTION, None)),
        out_specs=(by_head, P(None, SECTION, TENSOR)),
        check_vma=False,
    )
```

```python
import functools
import math

import jax
import jax.numpy as jnp
from jax import lax
from jax.experimental import pallas as pl
from jax.experimental.pallas import tpu as pltpu
from jax.sharding import Mesh, PartitionSpec as P

NBR_LEN = 128
HEAD = 128
GROUP = 64
PAIR = 2 * GROUP
ROWS = 256
BLOCK = 256
HALF = 4 * BLOCK
INV = 1.0 / math.sqrt(HEAD)
F32 = jnp.float32
BF16 = jnp.bfloat16

SECTION = ("zh", "y", "c")
TENSOR = ("z4", "z2", "x")
SPREAD = ("zh", "y", "c", "z4")
FLIP = [(0, 1), (1, 0)]


def across(k):
    return [(i, i ^ k) for i in range(4)]


def nt(a, b):
    return lax.dot_general(a, b, (((1,), (1,)), ((), ())), preferred_element_type=F32)


def nn(a, b):
    return jnp.dot(a, b, preferred_element_type=F32)


def cost(flops, nbytes):
    return pl.CostEstimate(flops=flops, bytes_accessed=nbytes, transcendentals=0)


def full(shape):
    return pl.BlockSpec(shape, lambda i, s: (0,) * len(shape))


VMEM = pl.BlockSpec(memory_space=pltpu.VMEM)
SMEM = pl.BlockSpec(memory_space=pltpu.SMEM)
LIMIT = pltpu.CompilerParams(vmem_limit_bytes=16 << 20)


def whole(kernel, n_args, out_shape, estimate):
    return pl.pallas_call(
        kernel,
        in_specs=[SMEM] + [VMEM] * n_args,
        out_specs=jax.tree.map(lambda _: VMEM, out_shape),
        out_shape=out_shape,
        cost_estimate=estimate,
        compiler_params=LIMIT,
    )


def streamed(kernel, in_specs, out_specs, out_shape, estimate, scratch=()):
    return pl.pallas_call(
        kernel,
        grid_spec=pltpu.PrefetchScalarGridSpec(
            num_scalar_prefetch=1,
            grid=(4,),
            in_specs=in_specs,
            out_specs=out_specs,
            scratch_shapes=scratch,
        ),
        out_shape=out_shape,
        cost_estimate=estimate,
        compiler_params=LIMIT,
    )


W_SPEC = pl.BlockSpec((1, 2, 4, BLOCK, HEAD), lambda i, s: (i, 0, 0, 0, 0))
E_SHAPE = (16, 4, 16, BLOCK)


def block_at(p, b):
    return pl.ds(pl.multiple_of(p * HALF + b * BLOCK, BLOCK), BLOCK)


def project_kernel(s_ref, q_ref, ct_ref, wk_ref, wv_ref, *out_refs):
    b = pl.program_id(0)
    for k in range(4):
        for p in range(2):
            key, value = (w[0, s_ref[0] ^ p, s_ref[1] ^ k] for w in (wk_ref, wv_ref))
            out_refs[k][0:GROUP, block_at(p, b)] = nt(q_ref[...], key).astype(BF16)
            out_refs[k][GROUP:PAIR, block_at(p, b)] = nt(ct_ref[...], value).astype(BF16)


def project(scalars, q, ct, wk, wv):
    small = full((GROUP, HEAD))
    return streamed(
        project_kernel,
        [small, small, W_SPEC, W_SPEC],
        [full((PAIR, 2 * HALF))] * 4,
        [jax.ShapeDtypeStruct((PAIR, 2 * HALF), BF16)] * 4,
        cost(2 * 128 * 8192 * 128, 6 << 20),
    )(scalars, q, ct, wk, wv)


def heads(a_refs, p, b):
    at = p * HALF + b * BLOCK
    return jnp.concatenate([r[:, at : at + BLOCK] for r in a_refs], axis=0)


def partial_scores(a_refs, e_ref, p):
    total = None
    for b in range(4):
        part = nt(heads(a_refs, p, b), e_ref[:, b].reshape(ROWS, BLOCK))
        total = part if total is None else total + part
    return total


def first_scores_kernel(s_ref, a0, a1, a2, a3, e_ref, out_ref):
    out_ref[...] = partial_scores((a0, a1, a2, a3), e_ref, 0)


def last_scores_kernel(s_ref, a0, a1, a2, a3, e_ref, first_ref, out_ref):
    total = first_ref[...] + partial_scores((a0, a1, a2, a3), e_ref, 1)
    for k in range(4):
        out_ref[s_ref[1] ^ k] = total[k * PAIR : (k + 1) * PAIR].astype(BF16)


HALF_COST = cost(2 * 512 * 1024 * 256, 2 << 20)


def first_scores(scalars, a, e):
    out = jax.ShapeDtypeStruct((4 * PAIR, ROWS), F32)
    return whole(first_scores_kernel, 5, out, HALF_COST)(scalars, *a, e)


def last_scores(scalars, a, e, first):
    out = jax.ShapeDtypeStruct((4, PAIR, ROWS), BF16)
    return whole(last_scores_kernel, 6, out, HALF_COST)(scalars, *a, e, first)


def attend_kernel(count_ref, s_ref, out_ref):
    total = s_ref[0].astype(F32)
    for k in range(1, 4):
        total = total + s_ref[k].astype(F32)
    scores = total[0:GROUP] * INV
    grad_probs = total[GROUP:PAIR]
    count = count_ref[0]
    row = lax.broadcasted_iota(jnp.int32, scores.shape, 1)
    weighted = jnp.where(row < count * NBR_LEN, jnp.exp(scores), 0.0)
    empty = jnp.where(count == 0, 1.0, 0.0)
    probs = weighted / (jnp.sum(weighted, axis=1, keepdims=True) + empty)
    centre = jnp.sum(probs * grad_probs, axis=1, keepdims=True)
    grad_scores = probs * (grad_probs - centre) * INV
    both = jnp.concatenate([grad_scores, probs], axis=0).T.astype(BF16)
    for k in range(4):
        out_ref[k] = both


def attend(counts, s):
    out = jax.ShapeDtypeStruct((4, ROWS, PAIR), BF16)
    return whole(attend_kernel, 1, out, cost(1 << 20, 1 << 19))(counts, s)


def term_kernel(p, s_ref, g_ref, a0, a1, a2, a3, out_ref):
    g = jnp.concatenate([g_ref[s_ref[1] ^ k] for k in range(4)], axis=1)
    for b in range(4):
        part = nn(g, heads((a0, a1, a2, a3), p, b))
        out_ref[:, b] = part.astype(out_ref.dtype).reshape(16, 16, BLOCK)


def term(scalars, g, a, p, kind):
    out = jax.ShapeDtypeStruct(E_SHAPE, kind)
    return whole(functools.partial(term_kernel, p), 5, out, HALF_COST)(scalars, g, *a)


def mix_kernel(s_ref, g_ref, own_ref, other_ref, *out_refs):
    gs = jnp.concatenate([g_ref[s_ref[1] ^ k, :, 0:GROUP] for k in range(4)], axis=1)
    gs = gs.astype(F32).T.astype(BF16)
    for p, e_ref in enumerate((own_ref, other_ref)):
        for b in range(4):
            part = nn(gs, e_ref[:, b].reshape(ROWS, BLOCK)).astype(BF16)
            at = p * HALF + b * BLOCK
            for k in range(4):
                out_refs[k][:, at : at + BLOCK] = part[k * GROUP : (k + 1) * GROUP]


def mix(scalars, g, own, other):
    out = [jax.ShapeDtypeStruct((GROUP, 2 * HALF), BF16)] * 4
    return whole(mix_kernel, 3, out, cost(2 * 256 * 256 * 2048, 2 << 20))(scalars, g, own, other)


def query_kernel(s_ref, x0, x1, x2, x3, w_ref, out_ref, acc_ref):
    b = pl.program_id(0)
    total = None
    for k, x_ref in enumerate((x0, x1, x2, x3)):
        for p in range(2):
            part = nn(x_ref[:, block_at(p, b)], w_ref[0, s_ref[0] ^ p, s_ref[1] ^ k])
            total = part if total is None else total + part

    @pl.when(b == 0)
    def _():
        acc_ref[...] = total

    @pl.when(b > 0)
    def _():
        acc_ref[...] += total

    @pl.when(b == 3)
    def _():
        out_ref[...] = acc_ref[...].astype(BF16)


def query(scalars, x, wk):
    return streamed(
        query_kernel,
        [full((GROUP, 2 * HALF))] * 4 + [W_SPEC],
        full((GROUP, HEAD)),
        jax.ShapeDtypeStruct((GROUP, HEAD), BF16),
        cost(2 * 64 * 8192 * 128, 3 << 20),
        [pltpu.VMEM((GROUP, HEAD), F32)],
    )(scalars, *x, wk)


def to_members(parts):
    return [parts[0]] + [lax.ppermute(parts[k], "x", across(k)) for k in range(1, 4)]


def local(encoded, w_key, w_value, queries, cotangent, counts):
    scalars = jnp.stack([lax.axis_index("z2"), lax.axis_index("x")]).astype(jnp.int32)
    wk = w_key.reshape(4, 2, 4, BLOCK, HEAD)
    wv = w_value.reshape(4, 2, 4, BLOCK, HEAD)
    out_rows = jnp.broadcast_to(encoded[:, None], (16, 4, 16, BLOCK)).reshape(64, 16, BLOCK)
    own = lax.all_to_all(out_rows, SPREAD, 0, 0, tiled=True).reshape(16, 4, 16, BLOCK)
    shared = to_members(project(scalars, queries[0], cotangent[0], wk, wv))
    other = lax.ppermute(own, "z2", FLIP)
    first = first_scores(scalars, shared, own)
    sums = last_scores(scalars, shared, other, first)
    parts = lax.all_to_all(sums, "x", 0, 0, tiled=True)
    grads = lax.all_to_all(attend(counts.reshape(1), parts), "x", 0, 0, tiled=True)
    passed = lax.ppermute(term(scalars, grads, shared, 1, BF16), "z2", FLIP)
    kept = term(scalars, grads, shared, 0, F32)
    mixture = mix(scalars, grads, own, other)
    kept, mixture = lax.optimization_barrier((kept, mixture))
    sent = (kept + passed.astype(F32)).astype(BF16).reshape(64, 16, BLOCK)
    terms = lax.all_to_all(sent, SPREAD, 0, 0, tiled=True).reshape(16, 4, 16, BLOCK)
    mixed = to_members(mixture)
    grad_queries = query(scalars, mixed, wk)
    grad_encoded = jnp.sum(terms.astype(F32), axis=1)
    return grad_queries[None], grad_encoded


def solution(mesh):
    fine = Mesh(mesh.devices.reshape(2, 4, 2, 4, 2, 4), ("zh", "y", "c", "z4", "z2", "x"))
    by_head = P(SECTION, None, TENSOR)
    return jax.shard_map(
        local,
        mesh=fine,
        in_specs=(P(None, SECTION, TENSOR), by_head, by_head, by_head, by_head, P(SECTION, None)),
        out_specs=(by_head, P(None, SECTION, TENSOR)),
        check_vma=False,
    )
```

```python
import functools
import math

import jax
import jax.numpy as jnp
from jax import lax
from jax.experimental import pallas as pl
from jax.experimental.pallas import tpu as pltpu
from jax.sharding import Mesh, PartitionSpec as P

NBR_LEN = 128
HEAD = 128
GROUP = 64
PAIR = 2 * GROUP
ROWS = 256
BLOCK = 256
HALF = 4 * BLOCK
INV = 1.0 / math.sqrt(HEAD)
F32 = jnp.float32
BF16 = jnp.bfloat16

SECTION = ("zh", "y", "c")
TENSOR = ("z4", "z2", "x")
FLIP = [(0, 1), (1, 0)]
COLUMN = ("zh", "y", "c", "z4", "z2")
SPREAD = [[2 * i + (w ^ (i // 32)) for i in range(64)] for w in range(2)]


def spread(blocks):
    out = lax.all_to_all(
        blocks.reshape(64, 16, BLOCK), COLUMN, 0, 0, axis_index_groups=SPREAD, tiled=True
    )
    return out.reshape(E_SHAPE)


def across(k):
    return [(i, i ^ k) for i in range(4)]


def nt(a, b):
    return lax.dot_general(a, b, (((1,), (1,)), ((), ())), preferred_element_type=F32)


def nn(a, b):
    return jnp.dot(a, b, preferred_element_type=F32)


def cost(flops, nbytes):
    return pl.CostEstimate(flops=flops, bytes_accessed=nbytes, transcendentals=0)


def full(shape):
    return pl.BlockSpec(shape, lambda i, s: (0,) * len(shape))


VMEM = pl.BlockSpec(memory_space=pltpu.VMEM)
SMEM = pl.BlockSpec(memory_space=pltpu.SMEM)
HBM = pl.BlockSpec(memory_space=pltpu.HBM)
LIMIT = pltpu.CompilerParams(vmem_limit_bytes=16 << 20)
ALONE = pltpu.CompilerParams(vmem_limit_bytes=62 << 20)


def whole(kernel, n_args, out_shape, estimate):
    return pl.pallas_call(
        kernel,
        in_specs=[SMEM] + [VMEM] * n_args,
        out_specs=jax.tree.map(lambda _: VMEM, out_shape),
        out_shape=out_shape,
        cost_estimate=estimate,
        compiler_params=LIMIT,
    )


def streamed(kernel, in_specs, out_specs, out_shape, estimate, scratch=()):
    return pl.pallas_call(
        kernel,
        grid_spec=pltpu.PrefetchScalarGridSpec(
            num_scalar_prefetch=1,
            grid=(4,),
            in_specs=in_specs,
            out_specs=out_specs,
            scratch_shapes=scratch,
        ),
        out_shape=out_shape,
        cost_estimate=estimate,
        compiler_params=LIMIT,
    )


W_SPEC = pl.BlockSpec((1, 2, 4, BLOCK, HEAD), lambda i, s: (i, 0, 0, 0, 0))
E_SHAPE = (16, 4, 16, BLOCK)


def block_at(p, b):
    return pl.ds(pl.multiple_of(p * HALF + b * BLOCK, BLOCK), BLOCK)


def project_kernel(s_ref, q_hbm, ct_hbm, wk_hbm, wv_hbm, o0, o1, o2, o3, rows, weights, sems):
    small = [
        pltpu.make_async_copy(src, rows.at[i], sems.at[8 + i])
        for i, src in enumerate((q_hbm, ct_hbm))
    ]
    large = [
        [pltpu.make_async_copy(w.at[b], weights.at[i, b], sems.at[2 * b + i]) for i, w in enumerate((wk_hbm, wv_hbm))]
        for b in range(4)
    ]
    for c in small + [c for pair in large for c in pair]:
        c.start()
    for c in small:
        c.wait()

    for b in range(4):
        for c in large[b]:
            c.wait()
        for k, out_ref in enumerate((o0, o1, o2, o3)):
            for p in range(2):
                at = slice(p * HALF + b * BLOCK, p * HALF + (b + 1) * BLOCK)
                for i in range(2):
                    part = nt(rows[i], weights[i, b, s_ref[0] ^ p, s_ref[1] ^ k])
                    out_ref[i * GROUP : (i + 1) * GROUP, at] = part.astype(BF16)


def project(scalars, q, ct, wk, wv):
    return pl.pallas_call(
        project_kernel,
        in_specs=[SMEM] + [HBM] * 4,
        out_specs=[VMEM] * 4,
        out_shape=[jax.ShapeDtypeStruct((PAIR, 2 * HALF), BF16)] * 4,
        scratch_shapes=[
            pltpu.VMEM((2, GROUP, HEAD), BF16),
            pltpu.VMEM((2, 4, 2, 4, BLOCK, HEAD), BF16),
            pltpu.SemaphoreType.DMA((10,)),
        ],
        cost_estimate=cost(2 * 128 * 8192 * 128, 6 << 20),
        compiler_params=ALONE,
    )(scalars, q, ct, wk, wv)


def heads(a_refs, p, b):
    at = p * HALF + b * BLOCK
    return jnp.concatenate([r[:, at : at + BLOCK] for r in a_refs], axis=0)


def partial_scores(a_refs, e_ref, p):
    total = None
    for b in range(4):
        part = jnp.concatenate(
            [nt(heads(a_refs, p ^ r, b), e_ref[8 * r : 8 * r + 8, b].reshape(128, BLOCK)) for r in range(2)],
            axis=1,
        )
        total = part if total is None else total + part
    return total


def first_scores_kernel(s_ref, a0, a1, a2, a3, e_ref, out_ref):
    out_ref[...] = partial_scores((a0, a1, a2, a3), e_ref, 0)


def last_scores_kernel(s_ref, a0, a1, a2, a3, e_ref, first_ref, out_ref):
    total = first_ref[...] + partial_scores((a0, a1, a2, a3), e_ref, 1)
    for k in range(4):
        out_ref[s_ref[1] ^ k] = total[k * PAIR : (k + 1) * PAIR].astype(BF16)


HALF_COST = cost(2 * 512 * 1024 * 256, 2 << 20)


def first_scores(scalars, a, e):
    out = jax.ShapeDtypeStruct((4 * PAIR, ROWS), F32)
    return whole(first_scores_kernel, 5, out, HALF_COST)(scalars, *a, e)


def last_scores(scalars, a, e, first):
    out = jax.ShapeDtypeStruct((4, PAIR, ROWS), BF16)
    return whole(last_scores_kernel, 6, out, HALF_COST)(scalars, *a, e, first)


def attend_kernel(count_ref, s_ref, out_ref):
    total = s_ref[0].astype(F32)
    for k in range(1, 4):
        total = total + s_ref[k].astype(F32)
    scores = total[0:GROUP] * INV
    grad_probs = total[GROUP:PAIR]
    count = count_ref[0]
    row = lax.broadcasted_iota(jnp.int32, scores.shape, 1)
    weighted = jnp.where(row < count * NBR_LEN, jnp.exp(scores), 0.0)
    empty = jnp.where(count == 0, 1.0, 0.0)
    probs = weighted / (jnp.sum(weighted, axis=1, keepdims=True) + empty)
    centre = jnp.sum(probs * grad_probs, axis=1, keepdims=True)
    grad_scores = probs * (grad_probs - centre) * INV
    both = jnp.concatenate([grad_scores, probs], axis=0).T.astype(BF16)
    for k in range(4):
        out_ref[k] = both


def attend(counts, s):
    out = jax.ShapeDtypeStruct((4, ROWS, PAIR), BF16)
    return whole(attend_kernel, 1, out, cost(1 << 20, 1 << 19))(counts, s)


def term_kernel(p, s_ref, g_ref, a0, a1, a2, a3, out_ref):
    g = jnp.concatenate([g_ref[s_ref[1] ^ k] for k in range(4)], axis=1)
    for r in range(2):
        for b in range(4):
            part = nn(g[128 * r : 128 * r + 128], heads((a0, a1, a2, a3), p ^ r, b))
            out_ref[8 * r : 8 * r + 8, b] = part.astype(out_ref.dtype).reshape(8, 16, BLOCK)


def term(scalars, g, a, p, kind):
    out = jax.ShapeDtypeStruct(E_SHAPE, kind)
    return whole(functools.partial(term_kernel, p), 5, out, HALF_COST)(scalars, g, *a)


def mix_kernel(s_ref, g_ref, own_ref, other_ref, *out_refs):
    gs = jnp.concatenate([g_ref[s_ref[1] ^ k, :, 0:GROUP] for k in range(4)], axis=1)
    gs = gs.astype(F32).T.astype(BF16)
    for p in range(2):
        halves = (own_ref, other_ref) if p == 0 else (other_ref, own_ref)
        for b in range(4):
            e = [h[8 * r : 8 * r + 8, b].reshape(128, BLOCK) for r, h in enumerate(halves)]
            part = nn(gs, jnp.concatenate(e, axis=0)).astype(BF16)
            at = p * HALF + b * BLOCK
            for k in range(4):
                out_refs[k][:, at : at + BLOCK] = part[k * GROUP : (k + 1) * GROUP]


def mix(scalars, g, own, other):
    out = [jax.ShapeDtypeStruct((GROUP, 2 * HALF), BF16)] * 4
    return whole(mix_kernel, 3, out, cost(2 * 256 * 256 * 2048, 2 << 20))(scalars, g, own, other)


def query_kernel(s_ref, x0, x1, x2, x3, w_ref, out_ref, acc_ref):
    b = pl.program_id(0)
    total = None
    for k, x_ref in enumerate((x0, x1, x2, x3)):
        for p in range(2):
            part = nn(x_ref[:, block_at(p, b)], w_ref[0, s_ref[0] ^ p, s_ref[1] ^ k])
            total = part if total is None else total + part

    @pl.when(b == 0)
    def _():
        acc_ref[...] = total

    @pl.when(b > 0)
    def _():
        acc_ref[...] += total

    @pl.when(b == 3)
    def _():
        out_ref[...] = acc_ref[...].astype(BF16)


def query(scalars, x, wk):
    return streamed(
        query_kernel,
        [full((GROUP, 2 * HALF))] * 4 + [W_SPEC],
        full((GROUP, HEAD)),
        jax.ShapeDtypeStruct((GROUP, HEAD), BF16),
        cost(2 * 64 * 8192 * 128, 3 << 20),
        [pltpu.VMEM((GROUP, HEAD), F32)],
    )(scalars, *x, wk)


def to_members(parts):
    return [parts[0]] + [lax.ppermute(parts[k], "x", across(k)) for k in range(1, 4)]


def local(encoded, w_key, w_value, queries, cotangent, counts):
    w = lax.axis_index("zh") ^ lax.axis_index("z2")
    scalars = jnp.stack([w, lax.axis_index("x")]).astype(jnp.int32)
    wk = w_key.reshape(4, 2, 4, BLOCK, HEAD)
    wv = w_value.reshape(4, 2, 4, BLOCK, HEAD)
    own = spread(jnp.broadcast_to(encoded[:, None], E_SHAPE))
    shared = to_members(project(scalars, queries[0], cotangent[0], wk, wv))
    other = lax.ppermute(own, "z2", FLIP)
    first = first_scores(scalars, shared, own)
    sums = last_scores(scalars, shared, other, first)
    parts = lax.all_to_all(sums, "x", 0, 0, tiled=True)
    grads = lax.all_to_all(attend(counts.reshape(1), parts), "x", 0, 0, tiled=True)
    passed = lax.ppermute(term(scalars, grads, shared, 1, BF16), "z2", FLIP)
    kept = term(scalars, grads, shared, 0, F32)
    mixture = mix(scalars, grads, own, other)
    kept, mixture = lax.optimization_barrier((kept, mixture))
    terms = spread((kept + passed.astype(F32)).astype(BF16))
    mixed = to_members(mixture)
    grad_queries = query(scalars, mixed, wk)
    grad_encoded = jnp.sum(terms.astype(F32), axis=1)
    return grad_queries[None], grad_encoded


def solution(mesh):
    fine = Mesh(mesh.devices.reshape(2, 4, 2, 4, 2, 4), ("zh", "y", "c", "z4", "z2", "x"))
    by_head = P(SECTION, None, TENSOR)
    return jax.shard_map(
        local,
        mesh=fine,
        in_specs=(P(None, SECTION, TENSOR), by_head, by_head, by_head, by_head, P(SECTION, None)),
        out_specs=(by_head, P(None, SECTION, TENSOR)),
        check_vma=False,
    )
```

```python
import functools
import math

import jax
import jax.numpy as jnp
from jax import lax
from jax.experimental import pallas as pl
from jax.experimental.pallas import tpu as pltpu
from jax.sharding import Mesh, PartitionSpec as P

NBR_LEN = 128
HEAD = 128
GROUP = 64
PAIR = 2 * GROUP
ROWS = 256
BLOCK = 256
SPAN = 2 * BLOCK
COLUMN = 4 * SPAN
INV = 1.0 / math.sqrt(HEAD)
F32 = jnp.float32
BF16 = jnp.bfloat16

AXES = {"zh": 2, "y": 4, "c": 2, "za": 2, "zb": 2, "z2": 2, "x": 4}
SECTION = ("zh", "y", "c")
TENSOR = ("za", "zb", "z2", "x")
QUAD = ("zb", "z2")

SPREAD_AXES = ("zh", "y", "c", "za", "zb", "z2")
ROW_GROUPS = [[4 * i + (w ^ (i // 16)) for i in range(32)] for w in range(4)]
TERM_GROUPS = [[2 * i + (w ^ (i // 32)) for i in range(64)] for w in range(2)]
E_SHAPE = (16, 2, 16, BLOCK)
T_SHAPE = (16, 4, 16, BLOCK)


def spread(blocks, groups):
    out = lax.all_to_all(
        blocks.reshape(-1, 16, BLOCK), SPREAD_AXES, 0, 0, axis_index_groups=groups, tiled=True
    )
    return out.reshape(blocks.shape)


def swap(array, axes, k):
    return lax.ppermute(array, axes, [(i, i ^ k) for i in range(4)])


def to_members(parts):
    two, one, three = [swap(parts[k], "x", k) for k in (2, 1, 3)]
    return [parts[0], one, two, three]


def nt(a, b):
    return lax.dot_general(a, b, (((1,), (1,)), ((), ())), preferred_element_type=F32)


def nn(a, b):
    return jnp.dot(a, b, preferred_element_type=F32)


def cost(flops, nbytes):
    return pl.CostEstimate(flops=flops, bytes_accessed=nbytes, transcendentals=0)


VMEM = pl.BlockSpec(memory_space=pltpu.VMEM)
SMEM = pl.BlockSpec(memory_space=pltpu.SMEM)
HBM = pl.BlockSpec(memory_space=pltpu.HBM)
LIMIT = pltpu.CompilerParams(vmem_limit_bytes=16 << 20)
ALONE = pltpu.CompilerParams(vmem_limit_bytes=62 << 20)


def whole(kernel, n_args, out_shape, estimate):
    return pl.pallas_call(
        kernel,
        in_specs=[SMEM] + [VMEM] * n_args,
        out_specs=jax.tree.map(lambda _: VMEM, out_shape),
        out_shape=out_shape,
        cost_estimate=estimate,
        compiler_params=LIMIT,
    )


def project_kernel(s_ref, q_hbm, ct_hbm, wk_hbm, wv_hbm, o0, o1, o2, o3, rows, weights, sems):
    small = [
        pltpu.make_async_copy(src, rows.at[i], sems.at[4 + i])
        for i, src in enumerate((q_hbm, ct_hbm))
    ]
    large = [
        [
            pltpu.make_async_copy(w.at[b], weights.at[i, b], sems.at[2 * b + i])
            for i, w in enumerate((wk_hbm, wv_hbm))
        ]
        for b in range(2)
    ]
    for c in small + large[0] + large[1]:
        c.start()
    for c in small:
        c.wait()
    for b in range(2):
        for c in large[b]:
            c.wait()
        for k, out_ref in enumerate((o0, o1, o2, o3)):
            for p in range(4):
                at = slice(p * SPAN + b * BLOCK, p * SPAN + (b + 1) * BLOCK)
                for i in range(2):
                    part = nt(rows[i], weights[i, b, s_ref[0] ^ p, s_ref[1] ^ k])
                    out_ref[i * GROUP : (i + 1) * GROUP, at] = part.astype(BF16)


def project(scalars, q, ct, wk, wv):
    return pl.pallas_call(
        project_kernel,
        in_specs=[SMEM] + [HBM] * 4,
        out_specs=[VMEM] * 4,
        out_shape=[jax.ShapeDtypeStruct((PAIR, COLUMN), BF16)] * 4,
        scratch_shapes=[
            pltpu.VMEM((2, GROUP, HEAD), BF16),
            pltpu.VMEM((2, 2, 4, 4, BLOCK, HEAD), BF16),
            pltpu.SemaphoreType.DMA((6,)),
        ],
        cost_estimate=cost(2 * 128 * 8192 * 128, 6 << 20),
        compiler_params=ALONE,
    )(scalars, q, ct, wk, wv)


def heads(a_refs, p):
    return jnp.concatenate([r[:, p * SPAN : (p + 1) * SPAN] for r in a_refs], axis=0)


def half_rows(e_ref, r):
    halves = [e_ref[8 * r : 8 * r + 8, b].reshape(128, BLOCK) for b in range(2)]
    return jnp.concatenate(halves, axis=1)


def scores_kernel(pieces, has_sum, last, s_ref, a0, a1, a2, a3, *refs):
    e_refs, out_ref = refs[: len(pieces)], refs[-1]
    sides = []
    for r in range(2):
        total = refs[len(pieces)][:, 128 * r : 128 * r + 128] if has_sum else None
        for j, e_ref in zip(pieces, e_refs, strict=True):
            part = nt(heads((a0, a1, a2, a3), j ^ r), half_rows(e_ref, r))
            total = part if total is None else total + part
        sides.append(total)
    for r in range(2):
        at = slice(128 * r, 128 * r + 128)
        if last:
            for k in range(4):
                out_ref[s_ref[1] ^ k, :, at] = sides[r][k * PAIR : (k + 1) * PAIR].astype(BF16)
        else:
            out_ref[:, at] = sides[r]


def scores(scalars, a, pieces, blocks, before, last):
    kernel = functools.partial(scores_kernel, pieces, before is not None, last)
    if last:
        out = jax.ShapeDtypeStruct((4, PAIR, ROWS), BF16)
    else:
        out = jax.ShapeDtypeStruct((4 * PAIR, ROWS), F32)
    args = (*a, *blocks) + (() if before is None else (before,))
    flops = len(pieces) * 2 * 512 * SPAN * ROWS
    return whole(kernel, len(args), out, cost(flops, 2 << 20))(scalars, *args)


def attend_kernel(count_ref, s_ref, out_ref):
    total = s_ref[0].astype(F32)
    for k in range(1, 4):
        total = total + s_ref[k].astype(F32)
    scores = total[0:GROUP] * INV
    grad_probs = total[GROUP:PAIR]
    count = count_ref[0]
    row = lax.broadcasted_iota(jnp.int32, scores.shape, 1)
    weighted = jnp.where(row < count * NBR_LEN, jnp.exp(scores), 0.0)
    empty = jnp.where(count == 0, 1.0, 0.0)
    probs = weighted / (jnp.sum(weighted, axis=1, keepdims=True) + empty)
    centre = jnp.sum(probs * grad_probs, axis=1, keepdims=True)
    grad_scores = probs * (grad_probs - centre) * INV
    both = jnp.concatenate([grad_scores, probs], axis=0).T.astype(BF16)
    for k in range(4):
        out_ref[k] = both


def attend(counts, s):
    out = jax.ShapeDtypeStruct((4, ROWS, PAIR), BF16)
    return whole(attend_kernel, 1, out, cost(1 << 20, 1 << 19))(counts, s)


def term_kernel(p2, s_ref, g_ref, a0, a1, a2, a3, out_ref):
    g = jnp.concatenate([g_ref[s_ref[1] ^ k] for k in range(4)], axis=1)
    for r in range(2):
        for pb in range(2):
            part = nn(g[128 * r : 128 * r + 128], heads((a0, a1, a2, a3), 2 * pb + (p2 ^ r)))
            for b in range(2):
                side = part[:, b * BLOCK : (b + 1) * BLOCK].astype(out_ref.dtype)
                zb = (s_ref[0] // 2) ^ pb
                out_ref[8 * r : 8 * r + 8, 2 * b + zb] = side.reshape(8, 16, BLOCK)


def term(scalars, g, a, p2, kind):
    out = jax.ShapeDtypeStruct(T_SHAPE, kind)
    kernel = functools.partial(term_kernel, p2)
    return whole(kernel, 5, out, cost(2 * 512 * 1024 * ROWS, 2 << 20))(scalars, g, *a)


def mix_kernel(s_ref, g_ref, e0, e1, e2, e3, *out_refs):
    gs = jnp.concatenate([g_ref[s_ref[1] ^ k, :, 0:GROUP] for k in range(4)], axis=1)
    gs = gs.astype(F32).T.astype(BF16)
    e_refs = (e0, e1, e2, e3)
    for p in range(4):
        e = jnp.concatenate([half_rows(e_refs[p ^ r], r) for r in range(2)], axis=0)
        part = nn(gs, e).astype(BF16)
        for k in range(4):
            out_refs[k][:, p * SPAN : (p + 1) * SPAN] = part[k * GROUP : (k + 1) * GROUP]


def mix(scalars, g, rows):
    out = [jax.ShapeDtypeStruct((GROUP, COLUMN), BF16)] * 4
    return whole(mix_kernel, 5, out, cost(2 * 256 * 256 * 2048, 2 << 20))(scalars, g, *rows)


def query_kernel(s_ref, x0, x1, x2, x3, w_ref, out_ref, acc_ref):
    b = pl.program_id(0)
    total = None
    for k, x_ref in enumerate((x0, x1, x2, x3)):
        for p in range(4):
            at = pl.ds(pl.multiple_of(p * SPAN + b * BLOCK, BLOCK), BLOCK)
            part = nn(x_ref[:, at], w_ref[0, s_ref[0] ^ p, s_ref[1] ^ k])
            total = part if total is None else total + part

    @pl.when(b == 0)
    def _():
        acc_ref[...] = total

    @pl.when(b == 1)
    def _():
        out_ref[...] = (acc_ref[...] + total).astype(BF16)


def query(scalars, x, wk):
    x_spec = pl.BlockSpec((GROUP, COLUMN), lambda i, s: (0, 0))
    return pl.pallas_call(
        query_kernel,
        grid_spec=pltpu.PrefetchScalarGridSpec(
            num_scalar_prefetch=1,
            grid=(2,),
            in_specs=[x_spec] * 4
            + [pl.BlockSpec((1, 4, 4, BLOCK, HEAD), lambda i, s: (i, 0, 0, 0, 0))],
            out_specs=pl.BlockSpec((GROUP, HEAD), lambda i, s: (0, 0)),
            scratch_shapes=[pltpu.VMEM((GROUP, HEAD), F32)],
        ),
        out_shape=jax.ShapeDtypeStruct((GROUP, HEAD), BF16),
        cost_estimate=cost(2 * 64 * 8192 * 128, 3 << 20),
        compiler_params=LIMIT,
    )(scalars, *x, wk)


def total_kernel(t_ref, out_ref):
    total = t_ref[:, 0].astype(F32)
    for b in range(1, 4):
        total = total + t_ref[:, b].astype(F32)
    out_ref[...] = total


def total_terms(terms):
    return pl.pallas_call(
        total_kernel,
        in_specs=[VMEM],
        out_specs=VMEM,
        out_shape=jax.ShapeDtypeStruct((16, 16, BLOCK), F32),
        cost_estimate=cost(1 << 18, 3 << 18),
        compiler_params=LIMIT,
    )(terms)


def local(encoded, w_key, w_value, queries, cotangent, counts):
    w = 2 * lax.axis_index("zb") + (lax.axis_index("zh") ^ lax.axis_index("z2"))
    scalars = jnp.stack([w, lax.axis_index("x")]).astype(jnp.int32)
    wk = w_key.reshape(2, 4, 4, BLOCK, HEAD)
    wv = w_value.reshape(2, 4, 4, BLOCK, HEAD)
    own = spread(jnp.broadcast_to(encoded[:, None], E_SHAPE), ROW_GROUPS)
    shared = to_members(project(scalars, queries[0], cotangent[0], wk, wv))
    rows = [own] + [swap(own, QUAD, j) for j in range(1, 4)]
    sums = scores(scalars, shared, (0, 1, 3), [rows[0], rows[1], rows[3]], None, False)
    sums = scores(scalars, shared, (2,), [rows[2]], sums, True)
    parts = lax.all_to_all(sums, "x", 0, 0, tiled=True)
    grads = lax.all_to_all(attend(counts.reshape(1), parts), "x", 0, 0, tiled=True)
    passed = swap(term(scalars, grads, shared, 1, BF16), QUAD, 1)
    kept = term(scalars, grads, shared, 0, F32)
    mixture = mix(scalars, grads, rows)
    kept, mixture = lax.optimization_barrier((kept, mixture))
    terms = spread((kept + passed.astype(F32)).astype(BF16), TERM_GROUPS)
    mixed = to_members(mixture)
    grad_queries = query(scalars, mixed, wk)
    grad_encoded = total_terms(terms)
    return grad_queries[None], grad_encoded


def solution(mesh):
    fine = Mesh(mesh.devices.reshape(tuple(AXES.values())), tuple(AXES))
    by_head = P(SECTION, None, TENSOR)
    return jax.shard_map(
        local,
        mesh=fine,
        in_specs=(P(None, SECTION, TENSOR), by_head, by_head, by_head, by_head, P(SECTION, None)),
        out_specs=(by_head, P(None, SECTION, TENSOR)),
        check_vma=False,
    )
```

```python
import functools
import math

import jax
import jax.numpy as jnp
from jax import lax
from jax.experimental import pallas as pl
from jax.experimental.pallas import tpu as pltpu
from jax.sharding import Mesh, PartitionSpec as P

NBR_LEN = 128
HEAD = 128
GROUP = 64
PAIR = 2 * GROUP
ROWS = 256
BLOCK = 256
SPAN = 2 * BLOCK
COLUMN = 4 * SPAN
INV = 1.0 / math.sqrt(HEAD)
F32 = jnp.float32
BF16 = jnp.bfloat16

AXES = {"zh": 2, "y": 4, "c": 2, "za": 2, "zb": 2, "z2": 2, "x": 4}
SECTION = ("zh", "y", "c")
TENSOR = ("za", "zb", "z2", "x")
QUAD = ("zb", "z2")

SPREAD_AXES = ("zh", "y", "c", "za", "zb", "z2")
ROW_GROUPS = [[4 * i + (w ^ (i // 16)) for i in range(32)] for w in range(4)]
TERM_GROUPS = [[2 * i + (w ^ (i // 32)) for i in range(64)] for w in range(2)]
E_SHAPE = (16, 2, 16, BLOCK)
T_SHAPE = (16, 4, 16, BLOCK)


def spread(blocks, groups):
    out = lax.all_to_all(
        blocks.reshape(-1, 16, BLOCK), SPREAD_AXES, 0, 0, axis_index_groups=groups, tiled=True
    )
    return out.reshape(blocks.shape)


def swap(array, axes, k):
    return lax.ppermute(array, axes, [(i, i ^ k) for i in range(4)])


def to_members(parts):
    two, one, three = [swap(parts[k], "x", k) for k in (2, 1, 3)]
    return [parts[0], one, two, three]


def nt(a, b):
    return lax.dot_general(a, b, (((1,), (1,)), ((), ())), preferred_element_type=F32)


def nn(a, b):
    return jnp.dot(a, b, preferred_element_type=F32)


def cost(flops, nbytes):
    return pl.CostEstimate(flops=flops, bytes_accessed=nbytes, transcendentals=0)


VMEM = pl.BlockSpec(memory_space=pltpu.VMEM)
SMEM = pl.BlockSpec(memory_space=pltpu.SMEM)
HBM = pl.BlockSpec(memory_space=pltpu.HBM)
LIMIT = pltpu.CompilerParams(vmem_limit_bytes=16 << 20)
ALONE = pltpu.CompilerParams(vmem_limit_bytes=62 << 20)


def whole(kernel, n_args, out_shape, estimate):
    return pl.pallas_call(
        kernel,
        in_specs=[SMEM] + [VMEM] * n_args,
        out_specs=jax.tree.map(lambda _: VMEM, out_shape),
        out_shape=out_shape,
        cost_estimate=estimate,
        compiler_params=LIMIT,
    )


def project_kernel(q_hbm, ct_hbm, wk_hbm, wv_hbm, o1, o2, o3, rows, weights, sems):
    w = 2 * lax.axis_index("zb") + (lax.axis_index("zh") ^ lax.axis_index("z2"))
    x = lax.axis_index("x")
    small = [
        pltpu.make_async_copy(src, rows.at[i], sems.at[4 + i])
        for i, src in enumerate((q_hbm, ct_hbm))
    ]
    large = [
        [
            pltpu.make_async_copy(src.at[b], weights.at[i, b], sems.at[2 * b + i])
            for i, src in enumerate((wk_hbm, wv_hbm))
        ]
        for b in range(2)
    ]
    for c in small + large[0] + large[1]:
        c.start()
    for c in small:
        c.wait()
    for b in range(2):
        for c in large[b]:
            c.wait()
        for k, out_ref in enumerate((o1, o2, o3), 1):
            for p in range(4):
                at = slice(p * SPAN + b * BLOCK, p * SPAN + (b + 1) * BLOCK)
                for i in range(2):
                    part = nt(rows[i], weights[i, b, w ^ p, x ^ k])
                    out_ref[i * GROUP : (i + 1) * GROUP, at] = part.astype(BF16)


def project(q, ct, wk, wv):
    return pl.pallas_call(
        project_kernel,
        in_specs=[HBM] * 4,
        out_specs=[VMEM] * 3,
        out_shape=[jax.ShapeDtypeStruct((PAIR, COLUMN), BF16)] * 3,
        scratch_shapes=[
            pltpu.VMEM((2, GROUP, HEAD), BF16),
            pltpu.VMEM((2, 2, 4, 4, BLOCK, HEAD), BF16),
            pltpu.SemaphoreType.DMA((6,)),
        ],
        cost_estimate=cost(2 * 128 * 6144 * 128, 6 << 20),
        compiler_params=ALONE,
    )(q, ct, wk, wv)


def project_own_kernel(s_ref, q_ref, ct_ref, wk_hbm, wv_hbm, out_ref, weights, sems):
    copies = [
        pltpu.make_async_copy(src.at[:, :, s_ref[1]], weights.at[i], sems.at[i])
        for i, src in enumerate((wk_hbm, wv_hbm))
    ]
    for c in copies:
        c.start()
    for i, r_ref in enumerate((q_ref, ct_ref)):
        copies[i].wait()
        for p in range(4):
            for b in range(2):
                at = slice(p * SPAN + b * BLOCK, p * SPAN + (b + 1) * BLOCK)
                part = nt(r_ref[...], weights[i, b, s_ref[0] ^ p])
                out_ref[i * GROUP : (i + 1) * GROUP, at] = part.astype(BF16)


def project_own(scalars, q, ct, wk, wv):
    return pl.pallas_call(
        project_own_kernel,
        in_specs=[SMEM, VMEM, VMEM, HBM, HBM],
        out_specs=VMEM,
        out_shape=jax.ShapeDtypeStruct((PAIR, COLUMN), BF16),
        scratch_shapes=[
            pltpu.VMEM((2, 2, 4, BLOCK, HEAD), BF16),
            pltpu.SemaphoreType.DMA((2,)),
        ],
        cost_estimate=cost(2 * 128 * 2048 * 128, 2 << 20),
        compiler_params=LIMIT,
    )(scalars, q, ct, wk, wv)


def heads(a_refs, p):
    return jnp.concatenate([r[:, p * SPAN : (p + 1) * SPAN] for r in a_refs], axis=0)


def half_rows(e_refs, j, r):
    if j < 2:
        halves = [e_refs[j][8 * r : 8 * r + 8, b] for b in range(2)]
    else:
        halves = [e_refs[2 * j - 2 + r][:, b] for b in range(2)]
    return jnp.concatenate([h.reshape(128, BLOCK) for h in halves], axis=1)


def scores_kernel(s_ref, a0, a1, a2, a3, *refs):
    e_refs, out_ref = refs[:-1], refs[-1]
    for r in range(2):
        total = None
        for j in range(4):
            part = nt(heads((a0, a1, a2, a3), j ^ r), half_rows(e_refs, j, r))
            total = part if total is None else total + part
        for k in range(4):
            at = slice(128 * r, 128 * r + 128)
            out_ref[s_ref[1] ^ k, :, at] = total[k * PAIR : (k + 1) * PAIR].astype(BF16)


def scores(scalars, a, rows):
    out = jax.ShapeDtypeStruct((4, PAIR, ROWS), BF16)
    estimate = cost(2 * 512 * 2048 * ROWS, 4 << 20)
    return whole(scores_kernel, 4 + len(rows), out, estimate)(scalars, *a, *rows)


def attend_kernel(count_ref, s_ref, out_ref):
    total = s_ref[0].astype(F32)
    for k in range(1, 4):
        total = total + s_ref[k].astype(F32)
    scores = total[0:GROUP] * INV
    grad_probs = total[GROUP:PAIR]
    count = count_ref[0]
    row = lax.broadcasted_iota(jnp.int32, scores.shape, 1)
    weighted = jnp.where(row < count * NBR_LEN, jnp.exp(scores), 0.0)
    empty = jnp.where(count == 0, 1.0, 0.0)
    probs = weighted / (jnp.sum(weighted, axis=1, keepdims=True) + empty)
    centre = jnp.sum(probs * grad_probs, axis=1, keepdims=True)
    grad_scores = probs * (grad_probs - centre) * INV
    both = jnp.concatenate([grad_scores, probs], axis=0).T.astype(BF16)
    for k in range(4):
        out_ref[k] = both


def attend(counts, s):
    out = jax.ShapeDtypeStruct((4, ROWS, PAIR), BF16)
    return whole(attend_kernel, 1, out, cost(1 << 20, 1 << 19))(counts, s)


def term_kernel(p2, s_ref, g_ref, a0, a1, a2, a3, out_ref):
    g = jnp.concatenate([g_ref[s_ref[1] ^ k] for k in range(4)], axis=1)
    for r in range(2):
        for pb in range(2):
            part = nn(g[128 * r : 128 * r + 128], heads((a0, a1, a2, a3), 2 * pb + (p2 ^ r)))
            for b in range(2):
                side = part[:, b * BLOCK : (b + 1) * BLOCK].astype(out_ref.dtype)
                zb = (s_ref[0] // 2) ^ pb
                out_ref[8 * r : 8 * r + 8, 2 * b + zb] = side.reshape(8, 16, BLOCK)


def term(scalars, g, a, p2, kind):
    out = jax.ShapeDtypeStruct(T_SHAPE, kind)
    kernel = functools.partial(term_kernel, p2)
    return whole(kernel, 5, out, cost(2 * 512 * 1024 * ROWS, 2 << 20))(scalars, g, *a)


def mix_kernel(s_ref, g_ref, *refs):
    e_refs, out_refs = refs[:6], refs[6:]
    gs = jnp.concatenate([g_ref[s_ref[1] ^ k, :, 0:GROUP] for k in range(4)], axis=1)
    gs = gs.astype(F32).T.astype(BF16)
    for p in range(4):
        e = jnp.concatenate([half_rows(e_refs, p ^ r, r) for r in range(2)], axis=0)
        part = nn(gs, e).astype(BF16)
        for k in range(4):
            out_refs[k][:, p * SPAN : (p + 1) * SPAN] = part[k * GROUP : (k + 1) * GROUP]


def mix(scalars, g, rows):
    out = [jax.ShapeDtypeStruct((GROUP, COLUMN), BF16)] * 4
    return whole(mix_kernel, 1 + len(rows), out, cost(2 * 256 * 256 * 2048, 2 << 20))(scalars, g, *rows)


def query_kernel(s_ref, x0, x1, x2, x3, w_ref, out_ref, acc_ref):
    b = pl.program_id(0)
    total = None
    for k, x_ref in enumerate((x0, x1, x2, x3)):
        for p in range(4):
            at = pl.ds(pl.multiple_of(p * SPAN + b * BLOCK, BLOCK), BLOCK)
            part = nn(x_ref[:, at], w_ref[0, s_ref[0] ^ p, s_ref[1] ^ k])
            total = part if total is None else total + part

    @pl.when(b == 0)
    def _():
        acc_ref[...] = total

    @pl.when(b == 1)
    def _():
        out_ref[...] = (acc_ref[...] + total).astype(BF16)


def query(scalars, x, wk):
    x_spec = pl.BlockSpec((GROUP, COLUMN), lambda i, s: (0, 0))
    return pl.pallas_call(
        query_kernel,
        grid_spec=pltpu.PrefetchScalarGridSpec(
            num_scalar_prefetch=1,
            grid=(2,),
            in_specs=[x_spec] * 4
            + [pl.BlockSpec((1, 4, 4, BLOCK, HEAD), lambda i, s: (i, 0, 0, 0, 0))],
            out_specs=pl.BlockSpec((GROUP, HEAD), lambda i, s: (0, 0)),
            scratch_shapes=[pltpu.VMEM((GROUP, HEAD), F32)],
        ),
        out_shape=jax.ShapeDtypeStruct((GROUP, HEAD), BF16),
        cost_estimate=cost(2 * 64 * 8192 * 128, 3 << 20),
        compiler_params=LIMIT,
    )(scalars, *x, wk)


def total_kernel(t_ref, out_ref):
    total = t_ref[:, 0].astype(F32)
    for b in range(1, 4):
        total = total + t_ref[:, b].astype(F32)
    out_ref[...] = total


def total_terms(terms):
    return pl.pallas_call(
        total_kernel,
        in_specs=[VMEM],
        out_specs=VMEM,
        out_shape=jax.ShapeDtypeStruct((16, 16, BLOCK), F32),
        cost_estimate=cost(1 << 18, 3 << 18),
        compiler_params=LIMIT,
    )(terms)


def local(encoded, w_key, w_value, queries, cotangent, counts):
    w = 2 * lax.axis_index("zb") + (lax.axis_index("zh") ^ lax.axis_index("z2"))
    scalars = jnp.stack([w, lax.axis_index("x")]).astype(jnp.int32)
    wk = w_key.reshape(2, 4, 4, BLOCK, HEAD)
    wv = w_value.reshape(2, 4, 4, BLOCK, HEAD)
    own = spread(jnp.broadcast_to(encoded[:, None], E_SHAPE), ROW_GROUPS)
    mine = (queries[0], cotangent[0], wk, wv)
    others = [swap(part, "x", k) for k, part in enumerate(project(*mine), 1)]
    third = [swap(own[8 * r : 8 * r + 8], QUAD, 3) for r in range(2)]
    rows = [own, swap(own, QUAD, 1), *[swap(t, QUAD, 1) for t in third], *third]
    mine, third = lax.optimization_barrier((mine, third))
    shared = [project_own(scalars, *mine), *others]
    rows = [*rows[:4], *third]
    sums = scores(scalars, shared, rows)
    parts = lax.all_to_all(sums, "x", 0, 0, tiled=True)
    grads = lax.all_to_all(attend(counts.reshape(1), parts), "x", 0, 0, tiled=True)
    passed = swap(term(scalars, grads, shared, 1, BF16), QUAD, 1)
    kept = term(scalars, grads, shared, 0, F32)
    mixture = mix(scalars, grads, rows)
    kept, mixture = lax.optimization_barrier((kept, mixture))
    terms = spread((kept + passed.astype(F32)).astype(BF16), TERM_GROUPS)
    mixed = to_members(mixture)
    grad_queries = query(scalars, mixed, wk)
    grad_encoded = total_terms(terms)
    return grad_queries[None], grad_encoded


def solution(mesh):
    fine = Mesh(mesh.devices.reshape(tuple(AXES.values())), tuple(AXES))
    by_head = P(SECTION, None, TENSOR)
    return jax.shard_map(
        local,
        mesh=fine,
        in_specs=(P(None, SECTION, TENSOR), by_head, by_head, by_head, by_head, P(SECTION, None)),
        out_specs=(by_head, P(None, SECTION, TENSOR)),
        check_vma=False,
    )
```

```python
import functools
import math

import jax
import jax.numpy as jnp
from jax import lax
from jax.experimental import pallas as pl
from jax.experimental.pallas import tpu as pltpu
from jax.sharding import Mesh, PartitionSpec as P

NBR_LEN = 128
HEAD = 128
GROUP = 64
PAIR = 2 * GROUP
ROWS = 256
BLOCK = 256
SPAN = 2 * BLOCK
COLUMN = 4 * SPAN
INV = 1.0 / math.sqrt(HEAD)
F32 = jnp.float32
BF16 = jnp.bfloat16

AXES = {"zh": 2, "y": 4, "c": 2, "za": 2, "zb": 2, "z2": 2, "x": 4}
SECTION = ("zh", "y", "c")
TENSOR = ("za", "zb", "z2", "x")
QUAD = ("zb", "z2")

SPREAD_AXES = ("zh", "y", "c", "za", "zb", "z2")
ROW_GROUPS = [[4 * i + (w ^ (i // 16)) for i in range(32)] for w in range(4)]
E_SHAPE = (16, 2, 16, BLOCK)


def spread(blocks, groups):
    out = lax.all_to_all(
        blocks.reshape(-1, 16, BLOCK), SPREAD_AXES, 0, 0, axis_index_groups=groups, tiled=True
    )
    return out.reshape(blocks.shape)


def swap(array, axes, k):
    return lax.ppermute(array, axes, [(i, i ^ k) for i in range(4)])


def to_members(parts):
    two, one, three = [swap(parts[k], "x", k) for k in (2, 1, 3)]
    return [parts[0], one, two, three]


def nt(a, b):
    return lax.dot_general(a, b, (((1,), (1,)), ((), ())), preferred_element_type=F32)


def nn(a, b):
    return jnp.dot(a, b, preferred_element_type=F32)


def cost(flops, nbytes):
    return pl.CostEstimate(flops=flops, bytes_accessed=nbytes, transcendentals=0)


VMEM = pl.BlockSpec(memory_space=pltpu.VMEM)
SMEM = pl.BlockSpec(memory_space=pltpu.SMEM)
HBM = pl.BlockSpec(memory_space=pltpu.HBM)
LIMIT = pltpu.CompilerParams(vmem_limit_bytes=16 << 20)
ALONE = pltpu.CompilerParams(vmem_limit_bytes=62 << 20)


def whole(kernel, n_args, out_shape, estimate):
    return pl.pallas_call(
        kernel,
        in_specs=[SMEM] + [VMEM] * n_args,
        out_specs=jax.tree.map(lambda _: VMEM, out_shape),
        out_shape=out_shape,
        cost_estimate=estimate,
        compiler_params=LIMIT,
    )


def project_kernel(q_hbm, ct_hbm, wk_hbm, wv_hbm, o1, o2, o3, rows, weights, sems):
    w = 2 * lax.axis_index("zb") + (lax.axis_index("zh") ^ lax.axis_index("z2"))
    x = lax.axis_index("x")
    small = [
        pltpu.make_async_copy(src, rows.at[i], sems.at[4 + i])
        for i, src in enumerate((q_hbm, ct_hbm))
    ]
    large = [
        [
            pltpu.make_async_copy(src.at[b], weights.at[i, b], sems.at[2 * b + i])
            for i, src in enumerate((wk_hbm, wv_hbm))
        ]
        for b in range(2)
    ]
    for c in small + large[0] + large[1]:
        c.start()
    for c in small:
        c.wait()
    for b in range(2):
        for c in large[b]:
            c.wait()
        for k, out_ref in enumerate((o1, o2, o3), 1):
            for p in range(4):
                at = slice(p * SPAN + b * BLOCK, p * SPAN + (b + 1) * BLOCK)
                for i in range(2):
                    part = nt(rows[i], weights[i, b, w ^ p, x ^ k])
                    out_ref[i * GROUP : (i + 1) * GROUP, at] = part.astype(BF16)


def project(q, ct, wk, wv):
    return pl.pallas_call(
        project_kernel,
        in_specs=[HBM] * 4,
        out_specs=[VMEM] * 3,
        out_shape=[jax.ShapeDtypeStruct((PAIR, COLUMN), BF16)] * 3,
        scratch_shapes=[
            pltpu.VMEM((2, GROUP, HEAD), BF16),
            pltpu.VMEM((2, 2, 4, 4, BLOCK, HEAD), BF16),
            pltpu.SemaphoreType.DMA((6,)),
        ],
        cost_estimate=cost(2 * 128 * 6144 * 128, 6 << 20),
        compiler_params=ALONE,
    )(q, ct, wk, wv)


def project_own_kernel(s_ref, q_ref, ct_ref, wk_hbm, wv_hbm, out_ref, weights, sems):
    copies = [
        pltpu.make_async_copy(src.at[:, :, s_ref[1]], weights.at[i], sems.at[i])
        for i, src in enumerate((wk_hbm, wv_hbm))
    ]
    for c in copies:
        c.start()
    for i, r_ref in enumerate((q_ref, ct_ref)):
        copies[i].wait()
        for p in range(4):
            for b in range(2):
                at = slice(p * SPAN + b * BLOCK, p * SPAN + (b + 1) * BLOCK)
                part = nt(r_ref[...], weights[i, b, s_ref[0] ^ p])
                out_ref[i * GROUP : (i + 1) * GROUP, at] = part.astype(BF16)


def project_own(scalars, q, ct, wk, wv):
    return pl.pallas_call(
        project_own_kernel,
        in_specs=[SMEM, VMEM, VMEM, HBM, HBM],
        out_specs=VMEM,
        out_shape=jax.ShapeDtypeStruct((PAIR, COLUMN), BF16),
        scratch_shapes=[
            pltpu.VMEM((2, 2, 4, BLOCK, HEAD), BF16),
            pltpu.SemaphoreType.DMA((2,)),
        ],
        cost_estimate=cost(2 * 128 * 2048 * 128, 2 << 20),
        compiler_params=LIMIT,
    )(scalars, q, ct, wk, wv)


def heads(a_refs, p):
    return jnp.concatenate([r[:, p * SPAN : (p + 1) * SPAN] for r in a_refs], axis=0)


def half_rows(e_refs, j, r):
    if j < 2:
        halves = [e_refs[j][8 * r : 8 * r + 8, b] for b in range(2)]
    else:
        halves = [e_refs[2 * j - 2 + r][:, b] for b in range(2)]
    return jnp.concatenate([h.reshape(128, BLOCK) for h in halves], axis=1)


def scores_kernel(s_ref, a0, a1, a2, a3, *refs):
    e_refs, out_ref = refs[:-1], refs[-1]
    for r in range(2):
        total = None
        for j in range(4):
            part = nt(heads((a0, a1, a2, a3), j ^ r), half_rows(e_refs, j, r))
            total = part if total is None else total + part
        for k in range(4):
            at = slice(128 * r, 128 * r + 128)
            out_ref[s_ref[1] ^ k, :, at] = total[k * PAIR : (k + 1) * PAIR].astype(BF16)


def scores(scalars, a, rows):
    out = jax.ShapeDtypeStruct((4, PAIR, ROWS), BF16)
    estimate = cost(2 * 512 * 2048 * ROWS, 4 << 20)
    return whole(scores_kernel, 4 + len(rows), out, estimate)(scalars, *a, *rows)


def attend_kernel(count_ref, s_ref, out_ref):
    total = s_ref[0].astype(F32)
    for k in range(1, 4):
        total = total + s_ref[k].astype(F32)
    scores = total[0:GROUP] * INV
    grad_probs = total[GROUP:PAIR]
    count = count_ref[0]
    row = lax.broadcasted_iota(jnp.int32, scores.shape, 1)
    weighted = jnp.where(row < count * NBR_LEN, jnp.exp(scores), 0.0)
    empty = jnp.where(count == 0, 1.0, 0.0)
    probs = weighted / (jnp.sum(weighted, axis=1, keepdims=True) + empty)
    centre = jnp.sum(probs * grad_probs, axis=1, keepdims=True)
    grad_scores = probs * (grad_probs - centre) * INV
    both = jnp.concatenate([grad_scores, probs], axis=0).T.astype(BF16)
    for k in range(4):
        out_ref[k] = both


def attend(counts, s):
    out = jax.ShapeDtypeStruct((4, ROWS, PAIR), BF16)
    return whole(attend_kernel, 1, out, cost(1 << 20, 1 << 19))(counts, s)


def term_kernel(pieces, s_ref, g_ref, a0, a1, a2, a3, *out_refs):
    g = jnp.concatenate([g_ref[s_ref[1] ^ k] for k in range(4)], axis=1)
    for j, out_ref in zip(pieces, out_refs, strict=True):
        for r in range(2):
            part = nn(g[128 * r : 128 * r + 128], heads((a0, a1, a2, a3), j ^ r))
            for b in range(2):
                side = part[:, b * BLOCK : (b + 1) * BLOCK].astype(out_ref.dtype)
                out_ref[8 * r : 8 * r + 8, b] = side.reshape(8, 16, BLOCK)


def term(scalars, g, a, pieces, kind):
    out = [jax.ShapeDtypeStruct(E_SHAPE, kind)] * len(pieces)
    kernel = functools.partial(term_kernel, pieces)
    flops = len(pieces) * 2 * 512 * SPAN * ROWS
    return whole(kernel, 5, out, cost(flops, 2 << 20))(scalars, g, *a)


def mix_kernel(s_ref, g_ref, *refs):
    e_refs, out_refs = refs[:6], refs[6:]
    gs = jnp.concatenate([g_ref[s_ref[1] ^ k, :, 0:GROUP] for k in range(4)], axis=1)
    gs = gs.astype(F32).T.astype(BF16)
    for p in range(4):
        e = jnp.concatenate([half_rows(e_refs, p ^ r, r) for r in range(2)], axis=0)
        part = nn(gs, e).astype(BF16)
        for k in range(4):
            out_refs[k][:, p * SPAN : (p + 1) * SPAN] = part[k * GROUP : (k + 1) * GROUP]


def mix(scalars, g, rows):
    out = [jax.ShapeDtypeStruct((GROUP, COLUMN), BF16)] * 4
    return whole(mix_kernel, 1 + len(rows), out, cost(2 * 256 * 256 * 2048, 2 << 20))(scalars, g, *rows)


def query_kernel(s_ref, x0, x1, x2, x3, w_ref, out_ref, acc_ref):
    b = pl.program_id(0)
    total = None
    for k, x_ref in enumerate((x0, x1, x2, x3)):
        for p in range(4):
            at = pl.ds(pl.multiple_of(p * SPAN + b * BLOCK, BLOCK), BLOCK)
            part = nn(x_ref[:, at], w_ref[0, s_ref[0] ^ p, s_ref[1] ^ k])
            total = part if total is None else total + part

    @pl.when(b == 0)
    def _():
        acc_ref[...] = total

    @pl.when(b == 1)
    def _():
        out_ref[...] = (acc_ref[...] + total).astype(BF16)


def query(scalars, x, wk):
    x_spec = pl.BlockSpec((GROUP, COLUMN), lambda i, s: (0, 0))
    return pl.pallas_call(
        query_kernel,
        grid_spec=pltpu.PrefetchScalarGridSpec(
            num_scalar_prefetch=1,
            grid=(2,),
            in_specs=[x_spec] * 4
            + [pl.BlockSpec((1, 4, 4, BLOCK, HEAD), lambda i, s: (i, 0, 0, 0, 0))],
            out_specs=pl.BlockSpec((GROUP, HEAD), lambda i, s: (0, 0)),
            scratch_shapes=[pltpu.VMEM((GROUP, HEAD), F32)],
        ),
        out_shape=jax.ShapeDtypeStruct((GROUP, HEAD), BF16),
        cost_estimate=cost(2 * 64 * 8192 * 128, 3 << 20),
        compiler_params=LIMIT,
    )(scalars, *x, wk)


def total_kernel(t_ref, out_ref):
    total = t_ref[:, 0].astype(F32)
    for b in range(1, 2):
        total = total + t_ref[:, b].astype(F32)
    out_ref[...] = total


def total_terms(terms):
    return pl.pallas_call(
        total_kernel,
        in_specs=[VMEM],
        out_specs=VMEM,
        out_shape=jax.ShapeDtypeStruct((16, 16, BLOCK), F32),
        cost_estimate=cost(1 << 18, 3 << 18),
        compiler_params=LIMIT,
    )(terms)


def local(encoded, w_key, w_value, queries, cotangent, counts):
    w = 2 * lax.axis_index("zb") + (lax.axis_index("zh") ^ lax.axis_index("z2"))
    scalars = jnp.stack([w, lax.axis_index("x")]).astype(jnp.int32)
    wk = w_key.reshape(2, 4, 4, BLOCK, HEAD)
    wv = w_value.reshape(2, 4, 4, BLOCK, HEAD)
    own = spread(jnp.broadcast_to(encoded[:, None], E_SHAPE), ROW_GROUPS)
    mine = (queries[0], cotangent[0], wk, wv)
    others = [swap(part, "x", k) for k, part in enumerate(project(*mine), 1)]
    third = [swap(own[8 * r : 8 * r + 8], QUAD, 3) for r in range(2)]
    rows = [own, swap(own, QUAD, 1), *[swap(t, QUAD, 1) for t in third], *third]
    mine, own = lax.optimization_barrier((mine, own))
    shared = [project_own(scalars, *mine), *others]
    rows = [own, *rows[1:]]
    sums = scores(scalars, shared, rows)
    parts = lax.all_to_all(sums, "x", 0, 0, tiled=True)
    grads = lax.all_to_all(attend(counts.reshape(1), parts), "x", 0, 0, tiled=True)
    far, near, third = term(scalars, grads, shared, (2, 1, 3), BF16)
    far, near = swap(far, QUAD, 1), swap(near, QUAD, 1)
    mixture = mix(scalars, grads, rows)
    far, mixture = lax.optimization_barrier((far, mixture))
    third = swap((third.astype(F32) + far.astype(F32)).astype(BF16), QUAD, 3)
    kept = term(scalars, grads, shared, (0,), F32)[0]
    sent = (kept + near.astype(F32) + third.astype(F32)).astype(BF16)
    mixed = to_members(mixture)
    sent, mixed[3] = lax.optimization_barrier((sent, mixed[3]))
    terms = spread(sent, ROW_GROUPS)
    grad_queries = query(scalars, mixed, wk)
    grad_encoded = total_terms(terms)
    return grad_queries[None], grad_encoded


def solution(mesh):
    fine = Mesh(mesh.devices.reshape(tuple(AXES.values())), tuple(AXES))
    by_head = P(SECTION, None, TENSOR)
    return jax.shard_map(
        local,
        mesh=fine,
        in_specs=(P(None, SECTION, TENSOR), by_head, by_head, by_head, by_head, P(SECTION, None)),
        out_specs=(by_head, P(None, SECTION, TENSOR)),
        check_vma=False,
    )
```

```python
import functools
import math

import jax
import jax.numpy as jnp
from jax import lax
from jax.experimental import pallas as pl
from jax.experimental.pallas import tpu as pltpu
from jax.sharding import Mesh, PartitionSpec as P

NBR_LEN = 128
HEAD = 128
GROUP = 64
PAIR = 2 * GROUP
ROWS = 256
BLOCK = 256
SPAN = 2 * BLOCK
COLUMN = 4 * SPAN
INV = 1.0 / math.sqrt(HEAD)
F32 = jnp.float32
BF16 = jnp.bfloat16

AXES = {"zh": 2, "y": 4, "c": 2, "za": 2, "zb": 2, "z2": 2, "x": 4}
SECTION = ("zh", "y", "c")
TENSOR = ("za", "zb", "z2", "x")
QUAD = ("zb", "z2")

SPREAD_AXES = ("zh", "y", "c", "za", "zb", "z2")
ROW_GROUPS = [[4 * i + (w ^ (i // 16)) for i in range(32)] for w in range(4)]
E_SHAPE = (16, 2, 16, BLOCK)


def spread(blocks, groups):
    out = lax.all_to_all(
        blocks.reshape(-1, 16, BLOCK), SPREAD_AXES, 0, 0, axis_index_groups=groups, tiled=True
    )
    return out.reshape(blocks.shape)


def swap(array, axes, k):
    return lax.ppermute(array, axes, [(i, i ^ k) for i in range(4)])


def to_members(parts):
    two, one, three = [swap(parts[k], "x", k) for k in (2, 1, 3)]
    return [parts[0], one, two, three]


def nt(a, b):
    return lax.dot_general(a, b, (((1,), (1,)), ((), ())), preferred_element_type=F32)


def nn(a, b):
    return jnp.dot(a, b, preferred_element_type=F32)


def cost(flops, nbytes):
    return pl.CostEstimate(flops=flops, bytes_accessed=nbytes, transcendentals=0)


VMEM = pl.BlockSpec(memory_space=pltpu.VMEM)
SMEM = pl.BlockSpec(memory_space=pltpu.SMEM)
HBM = pl.BlockSpec(memory_space=pltpu.HBM)
LIMIT = pltpu.CompilerParams(vmem_limit_bytes=16 << 20)
ALONE = pltpu.CompilerParams(vmem_limit_bytes=62 << 20)


def whole(kernel, n_args, out_shape, estimate):
    return pl.pallas_call(
        kernel,
        in_specs=[SMEM] + [VMEM] * n_args,
        out_specs=jax.tree.map(lambda _: VMEM, out_shape),
        out_shape=out_shape,
        cost_estimate=estimate,
        compiler_params=LIMIT,
    )


def project_kernel(q_hbm, ct_hbm, wk_hbm, wv_hbm, o1, o2, o3, rows, weights, sems):
    w = 2 * lax.axis_index("zb") + (lax.axis_index("zh") ^ lax.axis_index("z2"))
    x = lax.axis_index("x")
    small = [
        pltpu.make_async_copy(src, rows.at[i], sems.at[4 + i])
        for i, src in enumerate((q_hbm, ct_hbm))
    ]
    large = [
        [
            pltpu.make_async_copy(src.at[b], weights.at[i, b], sems.at[2 * b + i])
            for i, src in enumerate((wk_hbm, wv_hbm))
        ]
        for b in range(2)
    ]
    for c in small + large[0] + large[1]:
        c.start()
    for c in small:
        c.wait()
    for b in range(2):
        for c in large[b]:
            c.wait()
        for k, out_ref in enumerate((o1, o2, o3), 1):
            for p in range(4):
                at = slice(p * SPAN + b * BLOCK, p * SPAN + (b + 1) * BLOCK)
                for i in range(2):
                    part = nt(rows[i], weights[i, b, w ^ p, x ^ k])
                    out_ref[i * GROUP : (i + 1) * GROUP, at] = part.astype(BF16)


def project(q, ct, wk, wv):
    return pl.pallas_call(
        project_kernel,
        in_specs=[HBM] * 4,
        out_specs=[VMEM] * 3,
        out_shape=[jax.ShapeDtypeStruct((PAIR, COLUMN), BF16)] * 3,
        scratch_shapes=[
            pltpu.VMEM((2, GROUP, HEAD), BF16),
            pltpu.VMEM((2, 2, 4, 4, BLOCK, HEAD), BF16),
            pltpu.SemaphoreType.DMA((6,)),
        ],
        cost_estimate=cost(2 * 128 * 6144 * 128, 6 << 20),
        compiler_params=ALONE,
    )(q, ct, wk, wv)


def project_own_kernel(s_ref, q_ref, ct_ref, wk_hbm, wv_hbm, out_ref, weights, sems):
    copies = [
        pltpu.make_async_copy(src.at[:, :, s_ref[1]], weights.at[i], sems.at[i])
        for i, src in enumerate((wk_hbm, wv_hbm))
    ]
    for c in copies:
        c.start()
    for i, r_ref in enumerate((q_ref, ct_ref)):
        copies[i].wait()
        for p in range(4):
            for b in range(2):
                at = slice(p * SPAN + b * BLOCK, p * SPAN + (b + 1) * BLOCK)
                part = nt(r_ref[...], weights[i, b, s_ref[0] ^ p])
                out_ref[i * GROUP : (i + 1) * GROUP, at] = part.astype(BF16)


def project_own(scalars, q, ct, wk, wv):
    return pl.pallas_call(
        project_own_kernel,
        in_specs=[SMEM, VMEM, VMEM, HBM, HBM],
        out_specs=VMEM,
        out_shape=jax.ShapeDtypeStruct((PAIR, COLUMN), BF16),
        scratch_shapes=[
            pltpu.VMEM((2, 2, 4, BLOCK, HEAD), BF16),
            pltpu.SemaphoreType.DMA((2,)),
        ],
        cost_estimate=cost(2 * 128 * 2048 * 128, 2 << 20),
        compiler_params=LIMIT,
    )(scalars, q, ct, wk, wv)


def heads(a_refs, p):
    return jnp.concatenate([r[:, p * SPAN : (p + 1) * SPAN] for r in a_refs], axis=0)


def half_rows(e_refs, j, r):
    if j < 2:
        halves = [e_refs[j][8 * r : 8 * r + 8, b] for b in range(2)]
    else:
        halves = [e_refs[2 * j - 2 + r][:, b] for b in range(2)]
    return jnp.concatenate([h.reshape(128, BLOCK) for h in halves], axis=1)


def scores_kernel(s_ref, a0, a1, a2, a3, *refs):
    e_refs, out_ref = refs[:-1], refs[-1]
    for r in range(2):
        total = None
        for j in range(4):
            part = nt(heads((a0, a1, a2, a3), j ^ r), half_rows(e_refs, j, r))
            total = part if total is None else total + part
        for k in range(4):
            at = slice(128 * r, 128 * r + 128)
            out_ref[s_ref[1] ^ k, :, at] = total[k * PAIR : (k + 1) * PAIR].astype(BF16)


def scores(scalars, a, rows):
    out = jax.ShapeDtypeStruct((4, PAIR, ROWS), BF16)
    estimate = cost(2 * 512 * 2048 * ROWS, 4 << 20)
    return whole(scores_kernel, 4 + len(rows), out, estimate)(scalars, *a, *rows)


def attend_kernel(count_ref, s_ref, out_ref):
    total = s_ref[0].astype(F32)
    for k in range(1, 4):
        total = total + s_ref[k].astype(F32)
    scores = total[0:GROUP] * INV
    grad_probs = total[GROUP:PAIR]
    count = count_ref[0]
    row = lax.broadcasted_iota(jnp.int32, scores.shape, 1)
    weighted = jnp.where(row < count * NBR_LEN, jnp.exp(scores), 0.0)
    empty = jnp.where(count == 0, 1.0, 0.0)
    probs = weighted / (jnp.sum(weighted, axis=1, keepdims=True) + empty)
    centre = jnp.sum(probs * grad_probs, axis=1, keepdims=True)
    grad_scores = probs * (grad_probs - centre) * INV
    both = jnp.concatenate([grad_scores, probs], axis=0).T.astype(BF16)
    for k in range(4):
        out_ref[k] = both


def attend(counts, s):
    out = jax.ShapeDtypeStruct((4, ROWS, PAIR), BF16)
    return whole(attend_kernel, 1, out, cost(1 << 20, 1 << 19))(counts, s)


def term_kernel(pieces, s_ref, g_ref, a0, a1, a2, a3, *out_refs):
    g = jnp.concatenate([g_ref[s_ref[1] ^ k] for k in range(4)], axis=1)
    for j, out_ref in zip(pieces, out_refs, strict=True):
        for r in range(2):
            part = nn(g[128 * r : 128 * r + 128], heads((a0, a1, a2, a3), j ^ r))
            for b in range(2):
                side = part[:, b * BLOCK : (b + 1) * BLOCK].astype(out_ref.dtype)
                out_ref[8 * r : 8 * r + 8, b] = side.reshape(8, 16, BLOCK)


def term(scalars, g, a, pieces, kind):
    out = [jax.ShapeDtypeStruct(E_SHAPE, kind)] * len(pieces)
    kernel = functools.partial(term_kernel, pieces)
    flops = len(pieces) * 2 * 512 * SPAN * ROWS
    return whole(kernel, 5, out, cost(flops, 2 << 20))(scalars, g, *a)


def mix_kernel(s_ref, g_ref, *refs):
    e_refs, out_refs = refs[:6], refs[6:]
    gs = jnp.concatenate([g_ref[s_ref[1] ^ k, :, 0:GROUP] for k in range(4)], axis=1)
    gs = gs.astype(F32).T.astype(BF16)
    for p in range(4):
        e = jnp.concatenate([half_rows(e_refs, p ^ r, r) for r in range(2)], axis=0)
        part = nn(gs, e).astype(BF16)
        for k in range(4):
            out_refs[k][:, p * SPAN : (p + 1) * SPAN] = part[k * GROUP : (k + 1) * GROUP]


def mix(scalars, g, rows):
    out = [jax.ShapeDtypeStruct((GROUP, COLUMN), BF16)] * 4
    return whole(mix_kernel, 1 + len(rows), out, cost(2 * 256 * 256 * 2048, 2 << 20))(scalars, g, *rows)


def query_kernel(s_ref, x0, x1, x2, x3, w_ref, out_ref, acc_ref):
    b = pl.program_id(0)
    total = None
    for k, x_ref in enumerate((x0, x1, x2, x3)):
        for p in range(4):
            at = pl.ds(pl.multiple_of(p * SPAN + b * BLOCK, BLOCK), BLOCK)
            part = nn(x_ref[:, at], w_ref[0, s_ref[0] ^ p, s_ref[1] ^ k])
            total = part if total is None else total + part

    @pl.when(b == 0)
    def _():
        acc_ref[...] = total

    @pl.when(b == 1)
    def _():
        out_ref[...] = (acc_ref[...] + total).astype(BF16)


def query(scalars, x, wk):
    x_spec = pl.BlockSpec((GROUP, COLUMN), lambda i, s: (0, 0))
    return pl.pallas_call(
        query_kernel,
        grid_spec=pltpu.PrefetchScalarGridSpec(
            num_scalar_prefetch=1,
            grid=(2,),
            in_specs=[x_spec] * 4
            + [pl.BlockSpec((1, 4, 4, BLOCK, HEAD), lambda i, s: (i, 0, 0, 0, 0))],
            out_specs=pl.BlockSpec((GROUP, HEAD), lambda i, s: (0, 0)),
            scratch_shapes=[pltpu.VMEM((GROUP, HEAD), F32)],
        ),
        out_shape=jax.ShapeDtypeStruct((GROUP, HEAD), BF16),
        cost_estimate=cost(2 * 64 * 8192 * 128, 3 << 20),
        compiler_params=LIMIT,
    )(scalars, *x, wk)


def total_kernel(t_ref, out_ref):
    total = t_ref[:, 0].astype(F32)
    for b in range(1, 2):
        total = total + t_ref[:, b].astype(F32)
    out_ref[...] = total


def total_terms(terms):
    return pl.pallas_call(
        total_kernel,
        in_specs=[VMEM],
        out_specs=VMEM,
        out_shape=jax.ShapeDtypeStruct((16, 16, BLOCK), F32),
        cost_estimate=cost(1 << 18, 3 << 18),
        compiler_params=LIMIT,
    )(terms)


def local(encoded, w_key, w_value, queries, cotangent, counts):
    w = 2 * lax.axis_index("zb") + (lax.axis_index("zh") ^ lax.axis_index("z2"))
    scalars = jnp.stack([w, lax.axis_index("x")]).astype(jnp.int32)
    wk = w_key.reshape(2, 4, 4, BLOCK, HEAD)
    wv = w_value.reshape(2, 4, 4, BLOCK, HEAD)
    own = spread(jnp.broadcast_to(encoded[:, None], E_SHAPE), ROW_GROUPS)
    mine = (queries[0], cotangent[0], wk, wv)
    others = [swap(part, "x", k) for k, part in enumerate(project(*mine), 1)]
    third = [swap(own[8 * r : 8 * r + 8], QUAD, 3) for r in range(2)]
    rows = [own, swap(own, QUAD, 1), *[swap(t, QUAD, 1) for t in third], *third]
    mine, own = lax.optimization_barrier((mine, own))
    shared = [project_own(scalars, *mine), *others]
    rows = [own, *rows[1:]]
    sums = scores(scalars, shared, rows)
    parts = lax.all_to_all(sums, "x", 0, 0, tiled=True)
    grads = lax.all_to_all(attend(counts.reshape(1), parts), "x", 0, 0, tiled=True)
    far, near, third = term(scalars, grads, shared, (2, 1, 3), BF16)
    far, near = swap(far, QUAD, 1), swap(near, QUAD, 1)
    mixture = mix(scalars, grads, rows)
    far, mixture = lax.optimization_barrier((far, mixture))
    third = swap((third.astype(F32) + far.astype(F32)).astype(BF16), QUAD, 3)
    kept = term(scalars, grads, shared, (0,), F32)[0]
    sent = (kept + near.astype(F32) + third.astype(F32)).astype(BF16)
    mixed = to_members(mixture)
    sent, mixed[1], mixed[3] = lax.optimization_barrier((sent, mixed[1], mixed[3]))
    terms = spread(sent, ROW_GROUPS)
    grad_queries = query(scalars, mixed, wk)
    grad_encoded = total_terms(terms)
    return grad_queries[None], grad_encoded


def solution(mesh):
    fine = Mesh(mesh.devices.reshape(tuple(AXES.values())), tuple(AXES))
    by_head = P(SECTION, None, TENSOR)
    return jax.shard_map(
        local,
        mesh=fine,
        in_specs=(P(None, SECTION, TENSOR), by_head, by_head, by_head, by_head, P(SECTION, None)),
        out_specs=(by_head, P(None, SECTION, TENSOR)),
        check_vma=False,
    )
```
